512 devices in a mesh: grp: 16 (over x, y_lo, core), blk: 32 (over z, y_hi).
Axes of the slice: x: 4, y: 8 (y_hi: 4, y_lo: 2; y = y_hi * 2 + y_lo), z: 8, core: 2. Of those that a mesh axis runs over, the one named last changes fastest.
Arguments:
- series: bfloat16 [32, 512, 49152], P('grp', None, 'blk')
- labels: int32 [32], replicated, may hold values from 0 to 3, as said below
- panel_owner: int32 [2], replicated, may hold values from 0 to 31
Outputs:
- connectome: bfloat16 [2, 256, 49152], P(None, 'grp', 'blk')
The draws below stay inside these ranges and needn't reach their ends.
Inputs may be any that keep to these rules, and one draw needn't show every extreme that they name: `labels`: group 0 holds exactly one subject, group 1 exactly max(4, 1), group 2 exactly max(8, 1), group 3 the rest; which subjects is drawn.
All inputs are finite; a program needn't handle non-finite values.
Results may differ from the reference program's by a relative error of at most 0.011.
Values may be sent and summed in bfloat16 or wider, within the bound.
A program may use at most 64 MiB of HBM per device.

```python
import math
import jax
import jax.numpy as jnp
from jax import lax

COLS_DEV = 1536
FRAMES = 512
PANEL = 256
STEPS = 2
COHORTS = 4
GRAY = 49152
SUBJECTS = 32
N_BLK = 32


def draw_series(key, part):
    keys = jax.random.split(jax.random.fold_in(key, 11), 5)
    shape_full = (SUBJECTS, FRAMES, COLS_DEV * N_BLK)
    shape_load = (SUBJECTS, 1, COLS_DEV * N_BLK)
    noise = jax.random.normal(keys[0], shape_full, jnp.float32)
    shared = jax.random.normal(keys[1], (SUBJECTS, FRAMES, 1), jnp.float32)
    scale = jnp.exp(jax.random.uniform(keys[3], shape_load, jnp.float32, 0.0, math.log(10.0)))
    loading = jax.random.uniform(keys[2], shape_load, jnp.float32, -2.0, 2.0)
    offset = jax.random.uniform(keys[4], shape_load, jnp.float32, -2.0, 2.0) * scale
    values = offset + scale * (noise + loading * shared)
    return values.astype(jnp.bfloat16)


def draw_labels(key, part):
    order = jax.random.permutation(jax.random.fold_in(key, 23), SUBJECTS)
    second = max(SUBJECTS // 8, 1)
    third = max(SUBJECTS // 4, 1)
    label = (order >= 1).astype(jnp.int32) + (order >= 1 + second).astype(jnp.int32) + (order >= 1 + second + third).astype(jnp.int32)
    return label.astype(jnp.int32)


def setup_inputs(seed: int = 0) -> dict:
    splits = jax.random.split(jax.random.key(seed), 4)
    return {
        "series": draw_series(jax.random.fold_in(splits[3], 71), 0),
        "labels": draw_labels(jax.random.fold_in(splits[3], 71), 0),
        "panel_owner": jax.random.randint(splits[2], (STEPS,), 0, N_BLK).astype(jnp.int32),
    }


epsilon = 1e-05
clip_limit = 0.99

def standardize(values):
    values = values.astype(jnp.float32)
    center = lax.optimization_barrier(jnp.mean(values, axis=0, keepdims=True))
    centred = values - center
    spread = lax.optimization_barrier(jnp.mean(centred * centred, axis=0, keepdims=True))
    return (centred * lax.rsqrt(spread + epsilon)).astype(jnp.bfloat16)

def fisher_z(correl):
    bounded = jnp.clip(correl, -clip_limit, clip_limit)
    return 0.5 * jnp.log((1.0 + bounded) / (1.0 - bounded))

def reference(series, labels, panel_owner):
    onehot = (labels[:, None] == jnp.arange(COHORTS, dtype=jnp.int32)[None, :]).astype(jnp.float32)
    counts = lax.optimization_barrier(jnp.sum(onehot, axis=0))
    weight = lax.optimization_barrier(jnp.sum(onehot / (COHORTS * counts)[None, :], axis=1))
    starts = (panel_owner * COLS_DEV + jnp.arange(STEPS, dtype=jnp.int32) * PANEL).astype(jnp.int32)

    def one_subject(running, item):
        values, single_weight = item
        scored = standardize(values)
        stacked = []
        for step_index in range(STEPS):
            panel = lax.dynamic_slice_in_dim(scored, starts[step_index], PANEL, 1)
            correl = jnp.dot(panel.T, scored, preferred_element_type=jnp.float32) / float(FRAMES)
            stacked.append(fisher_z(correl))
        return (running + single_weight * jnp.stack(stacked), None)
    summed, _ = lax.scan(one_subject, jnp.zeros((STEPS, PANEL, GRAY), jnp.float32), (series, weight))
    column_block = (jnp.arange(GRAY, dtype=jnp.int32) // COLS_DEV).astype(jnp.int32)
    upper = column_block[None, None, :] >= panel_owner[:, None, None]
    return jnp.where(upper, summed, jnp.zeros_like(summed)).astype(jnp.bfloat16)
```

```python
import functools

import jax
import jax.numpy as jnp
from jax import lax
from jax.experimental import pallas as pl
from jax.experimental.pallas import tpu as pltpu
from jax.sharding import PartitionSpec as P

MESH = pl.DeviceIdType.MESH
STEPS, PANEL, COHORTS, MEMBERS = 2, 256, 4, 2
FRAMES, COLUMNS = 512, 1536
NZ, NY, NQ, NC = 8, 4, 8, 2
N_GRP, N_BLK = NQ * NC, NZ * NY
CHUNK = MEMBERS * PANEL // NZ
PIECE = CHUNK // NY
OUT_ROWS = PANEL // N_GRP
TILE = 256
ROWS = 128
epsilon = 1e-05
clip_limit = 0.99

N_COPIES = STEPS * (7 + 6 + 7 + 1 + 7)


def kernel(
    labels_ref, owner_ref, series_ref, out_ref,
    raw, scored, panel, land_a, mid, land_b, whole, part, land_e, half, land_h,
    load_sem, send_sem, recv_sem,
):
    grp, blk = lax.axis_index("grp"), lax.axis_index("blk")
    zi, yi = blk // NY, blk % NY
    qi, core = grp // NC, grp % NC

    def at_z(offset):
        return {"blk": ((zi + offset + NZ) % NZ) * NY + yi}

    def at_y(offset):
        return {"blk": zi * NY + (yi + offset) % NY}

    def at_q(offset):
        return {"grp": ((qi + offset) % NQ) * NC + core}

    other_core = {"grp": qi * NC + 1 - core}

    loads = []
    for k, (start, width) in enumerate(
        [(0, PANEL), (PANEL, PANEL), (STEPS * PANEL, COLUMNS - STEPS * PANEL)]
    ):
        window = (slice(None), slice(None), pl.ds(start, width))
        loads.append(
            pltpu.make_async_copy(series_ref.at[window], raw.at[window], load_sem.at[k])
        )
        loads[-1].start()

    barrier = pltpu.get_barrier_semaphore()
    peers = [at_z(1), at_z(-1)]
    peers += [at_y(o) for o in range(1, NY)]
    peers += [other_core]
    peers += [at_q(o) for o in range(1, NQ)]
    for peer in peers:
        pl.semaphore_signal(barrier, inc=1, device_id=peer, device_id_type=MESH)

    count = [0]

    def send(src, dst, device):
        k = count[0]
        count[0] += 1
        copy = pltpu.make_async_remote_copy(
            src_ref=src,
            dst_ref=dst,
            send_sem=send_sem.at[k],
            recv_sem=recv_sem.at[k],
            device_id=device,
            device_id_type=MESH,
        )
        copy.start()
        return copy

    started = []

    def standardize(s, start, step):
        cols = pl.ds(start, TILE)
        total = jnp.zeros((8, TILE), jnp.float32)
        for r in range(0, FRAMES, ROWS):
            x = raw[s, pl.ds(r, ROWS), cols].astype(jnp.float32)
            total += jnp.sum(x.reshape(ROWS // 8, 8, TILE), axis=0)
        center = jnp.sum(total, axis=0, keepdims=True) * (1.0 / FRAMES)
        total = jnp.zeros((8, TILE), jnp.float32)
        for r in range(0, FRAMES, ROWS):
            x = raw[s, pl.ds(r, ROWS), cols].astype(jnp.float32) - center
            total += jnp.sum((x * x).reshape(ROWS // 8, 8, TILE), axis=0)
        spread = jnp.sum(total, axis=0, keepdims=True) * (1.0 / FRAMES)
        scale = lax.rsqrt(spread + epsilon)
        for r in range(0, FRAMES, ROWS):
            x = raw[s, pl.ds(r, ROWS), cols].astype(jnp.float32) - center
            y = x * scale
            scored[s, pl.ds(r, ROWS), cols] = y.astype(jnp.bfloat16)
            if step is not None:
                mine = jnp.where(owner_ref[step] == blk, 1.0, 0.0)
                turned = (y * mine).T.astype(jnp.bfloat16)
                per = PANEL // CHUNK
                panel[step, pl.ds(s * per, per), :, pl.ds(r, ROWS)] = turned.reshape(
                    per, CHUNK, ROWS
                )

    rest = [
        (s, c) for s in range(MEMBERS) for c in range(STEPS * PANEL, COLUMNS, TILE)
    ]

    def some_rest(n):
        for _ in range(n):
            if rest:
                standardize(*rest.pop(0), None)

    def hops(k, sign):
        return 4 if (sign > 0) == (k == 0) else 3

    a_copies = {}

    def send_a(k, sign, t):
        reach = hops(k, sign)
        d = (zi + sign * (reach - t) + NZ) % NZ
        way = 0 if sign > 0 else 1
        if t == 0:
            src = panel.at[k, d]
        else:
            a_copies[k, sign, t - 1].wait_recv()
            src = land_a.at[k, way, t - 1]
            src[...] += panel[k, d]
        a_copies[k, sign, t] = send(src, land_a.at[k, way, t], at_z(sign))

    for k in range(STEPS):
        loads[k].wait()
        for s in range(MEMBERS):
            standardize(s, k * PANEL, k)
        if k == 0:
            pl.semaphore_wait(barrier, len(peers))
        for sign in (1, -1):
            send_a(k, sign, 0)
    loads[2].wait()
    for t in range(1, 4):
        some_rest(2)
        for k in range(STEPS):
            for sign in (1, -1):
                if t < hops(k, sign):
                    send_a(k, sign, t)
    some_rest(2)

    b_copies = {}
    for k in range(STEPS):
        for sign in (1, -1):
            a_copies[k, sign, hops(k, sign) - 1].wait_recv()
        got = [land_a[k, w, hops(k, sign) - 1] for w, sign in ((0, 1), (1, -1))]
        mid[k] = (panel[k, zi] + got[0] + got[1]).reshape(NY, PIECE, FRAMES)
        for o in (2, 1, 3):
            b_copies[k, o] = send(
                mid.at[k, (yi + o) % NY], land_b.at[k, o - 1], at_y(o)
            )
    g_copies = {}
    for k in range(STEPS):
        for o in range(1, NY):
            b_copies[k, o].wait_recv()
        whole[k, zi, yi] = mid[k, yi] + land_b[k, 0] + land_b[k, 1] + land_b[k, 2]
        for o in (2, 1, 3):
            g_copies[k, o] = send(
                whole.at[k, zi, yi], whole.at[k, zi, yi], at_y(o)
            )
    some_rest(8)

    c_copies = {}

    def send_c(k, sign, t):
        if t:
            c_copies[k, sign, t - 1].wait_recv()
        d = (zi - sign * t + NZ) % NZ
        c_copies[k, sign, t] = send(whole.at[k, d], whole.at[k, d], at_z(sign))

    for k in range(STEPS):
        for o in range(1, NY):
            g_copies[k, o].wait_recv()
        for sign in (1, -1):
            send_c(k, sign, 0)
    for t in range(1, 4):
        for k in range(STEPS):
            for sign in (1, -1):
                if t < hops(k, sign):
                    send_c(k, sign, t)

    halves = []
    for s in range(MEMBERS):
        label = labels_ref[grp * MEMBERS + s]
        same = jnp.int32(0)
        for i in range(N_GRP * MEMBERS):
            same += jnp.where(labels_ref[i] == label, 1, 0)
        counted = jnp.full((1, TILE), same.astype(jnp.float32))
        halves.append(0.5 / (COHORTS * counted))

    d_copies = {}
    for k in range(STEPS):
        for sign in (1, -1):
            c_copies[k, sign, hops(k, sign) - 1].wait_recv()

        def tile(j, carry, k=k):
            cols = pl.ds(pl.multiple_of(j * TILE, TILE), TILE)
            total = None
            per = NZ // MEMBERS
            for s in range(MEMBERS):
                rows = whole[k, pl.ds(s * per, per)].reshape(PANEL, FRAMES)
                q = jnp.dot(
                    rows, scored[s, :, cols], preferred_element_type=jnp.float32
                ) * (1.0 / FRAMES)
                q = jnp.clip(q, -clip_limit, clip_limit)
                term = halves[s] * jnp.log((1.0 + q) / (1.0 - q))
                total = term if total is None else total + term
            part[k, :, :, :, cols] = total.astype(jnp.bfloat16).reshape(
                NQ, NC, OUT_ROWS, TILE
            )
            return carry

        lax.fori_loop(0, COLUMNS // TILE, tile, 0)
        d_copies[k] = send(part.at[k, :, 1 - core], land_e.at[k], other_core)

    h_copies = {}
    for k in range(STEPS):
        d_copies[k].wait_recv()
        half[k] = (
            part[k, :, core].astype(jnp.float32) + land_e[k].astype(jnp.float32)
        ).astype(jnp.bfloat16)
        for o in (4, 3, 5, 2, 6, 1, 7):
            h_copies[k, o] = send(
                half.at[k, (qi + o) % NQ], land_h.at[k, o - 1], at_q(o)
            )
    for k in range(STEPS):
        total = half[k, qi].astype(jnp.float32)
        for o in range(1, NQ):
            h_copies[k, o].wait_recv()
            total += land_h[k, o - 1].astype(jnp.float32)
        out_ref[k] = total

    for copies in (a_copies, b_copies, g_copies, c_copies, d_copies, h_copies):
        for copy in copies.values():
            copy.wait_send()


def body(series, labels, panel_owner):
    half_type = jnp.bfloat16
    summed = pl.pallas_call(
        kernel,
        out_shape=jax.ShapeDtypeStruct((STEPS, OUT_ROWS, COLUMNS), jnp.float32),
        in_specs=[
            pl.BlockSpec(memory_space=pltpu.SMEM),
            pl.BlockSpec(memory_space=pltpu.SMEM),
            pl.BlockSpec(memory_space=pl.ANY),
        ],
        out_specs=pl.BlockSpec(memory_space=pltpu.VMEM),
        scratch_shapes=[
            pltpu.VMEM((MEMBERS, FRAMES, COLUMNS), half_type),
            pltpu.VMEM((MEMBERS, FRAMES, COLUMNS), half_type),
            pltpu.VMEM((STEPS, NZ, CHUNK, FRAMES), half_type),
            pltpu.VMEM((STEPS, 2, 4, CHUNK, FRAMES), half_type),
            pltpu.VMEM((STEPS, NY, PIECE, FRAMES), half_type),
            pltpu.VMEM((STEPS, NY - 1, PIECE, FRAMES), half_type),
            pltpu.VMEM((STEPS, NZ, NY, PIECE, FRAMES), half_type),
            pltpu.VMEM((STEPS, NQ, NC, OUT_ROWS, COLUMNS), half_type),
            pltpu.VMEM((STEPS, NQ, OUT_ROWS, COLUMNS), half_type),
            pltpu.VMEM((STEPS, NQ, OUT_ROWS, COLUMNS), half_type),
            pltpu.VMEM((STEPS, NQ - 1, OUT_ROWS, COLUMNS), half_type),
            pltpu.SemaphoreType.DMA((3,)),
            pltpu.SemaphoreType.DMA((N_COPIES,)),
            pltpu.SemaphoreType.DMA((N_COPIES,)),
        ],
        compiler_params=pltpu.CompilerParams(
            collective_id=0, has_side_effects=True, vmem_limit_bytes=40 * 1024 * 1024
        ),
    )(labels, panel_owner, series)
    upper = lax.axis_index("blk") >= panel_owner
    return jnp.where(upper[:, None, None], summed, 0.0).astype(jnp.bfloat16)


def solution(mesh):
    in_specs = (P("grp", None, "blk"), P(), P())
    out_specs = P(None, "grp", "blk")
    return jax.shard_map(body, mesh=mesh, in_specs=in_specs, out_specs=out_specs, check_vma=False)
```

```python
import functools

import jax
import jax.numpy as jnp
from jax import lax
from jax.experimental import pallas as pl
from jax.experimental.pallas import tpu as pltpu
from jax.sharding import PartitionSpec as P

MESH = pl.DeviceIdType.MESH
STEPS, PANEL, COHORTS, MEMBERS = 2, 256, 4, 2
FRAMES, COLUMNS = 512, 1536
NZ, NY, NQ, NC = 8, 4, 8, 2
N_GRP, N_BLK = NQ * NC, NZ * NY
CHUNK = MEMBERS * PANEL // NZ
PIECE = CHUNK // NY
SHARE = PANEL // NZ
OUT_ROWS = PANEL // N_GRP
TILE = 256
ROWS = 128
epsilon = 1e-05
clip_limit = 0.99

N_COPIES = STEPS * (7 + 6 + 7) + NQ + NQ - 1


def kernel(
    labels_hbm, owner_hbm, series_ref, out_ref,
    labels_ref, owner_ref, raw, scored, panel, land_a, mid, land_b, whole,
    part, land_e, half, land_h, load_sem, send_sem, recv_sem,
):
    grp, blk = lax.axis_index("grp"), lax.axis_index("blk")
    zi, yi = blk // NY, blk % NY
    qi, core = grp // NC, grp % NC

    def at_z(offset):
        return {"blk": ((zi + offset + NZ) % NZ) * NY + yi}

    def at_y(offset):
        return {"blk": zi * NY + (yi + offset) % NY}

    def at_q(offset):
        return {"grp": ((qi + offset) % NQ) * NC + core}

    other_core = {"grp": qi * NC + 1 - core}

    loads = []
    small = [
        pltpu.make_async_copy(owner_hbm, owner_ref, load_sem.at[3]),
        pltpu.make_async_copy(labels_hbm, labels_ref, load_sem.at[4]),
    ]
    for copy in small:
        copy.start()
    for k, (start, width) in enumerate(
        [(0, PANEL), (PANEL, PANEL), (STEPS * PANEL, COLUMNS - STEPS * PANEL)]
    ):
        window = (slice(None), slice(None), pl.ds(start, width))
        loads.append(
            pltpu.make_async_copy(series_ref.at[window], raw.at[window], load_sem.at[k])
        )
        loads[-1].start()

    barrier = pltpu.get_barrier_semaphore()
    peers = [at_z(1), at_z(-1)]
    peers += [at_y(o) for o in range(1, NY)]
    peers += [other_core]
    peers += [at_q(o) for o in range(1, NQ)]
    for peer in peers:
        pl.semaphore_signal(barrier, inc=1, device_id=peer, device_id_type=MESH)

    count = [0]

    def send(src, dst, device):
        k = count[0]
        count[0] += 1
        copy = pltpu.make_async_remote_copy(
            src_ref=src,
            dst_ref=dst,
            send_sem=send_sem.at[k],
            recv_sem=recv_sem.at[k],
            device_id=device,
            device_id_type=MESH,
        )
        copy.start()
        return copy

    def standardize(s, start, step):
        cols = pl.ds(start, TILE)
        total = jnp.zeros((8, TILE), jnp.float32)
        for r in range(0, FRAMES, ROWS):
            x = raw[s, pl.ds(r, ROWS), cols].astype(jnp.float32)
            total += jnp.sum(x.reshape(ROWS // 8, 8, TILE), axis=0)
        center = jnp.sum(total, axis=0, keepdims=True) * (1.0 / FRAMES)
        total = jnp.zeros((8, TILE), jnp.float32)
        for r in range(0, FRAMES, ROWS):
            x = raw[s, pl.ds(r, ROWS), cols].astype(jnp.float32) - center
            total += jnp.sum((x * x).reshape(ROWS // 8, 8, TILE), axis=0)
        spread = jnp.sum(total, axis=0, keepdims=True) * (1.0 / FRAMES)
        scale = lax.rsqrt(spread + epsilon)
        for r in range(0, FRAMES, ROWS):
            x = raw[s, pl.ds(r, ROWS), cols].astype(jnp.float32) - center
            y = x * scale
            scored[s, pl.ds(r, ROWS), cols] = y.astype(jnp.bfloat16)
            if step is not None:
                mine = jnp.where(owner_ref[step] == blk, 1.0, 0.0)
                turned = (y * mine).T.astype(jnp.bfloat16)
                panel[step, :, pl.ds(s * SHARE, SHARE), pl.ds(r, ROWS)] = turned.reshape(
                    NZ, SHARE, ROWS
                )

    rest = [
        (s, c) for s in range(MEMBERS) for c in range(STEPS * PANEL, COLUMNS, TILE)
    ]

    def some_rest(n):
        for _ in range(n):
            if rest:
                standardize(*rest.pop(0), None)

    def hops(k, sign):
        return 4 if (sign > 0) == (k == 0) else 3

    a_copies = {}

    def send_a(k, sign, t):
        reach = hops(k, sign)
        d = (zi + sign * (reach - t) + NZ) % NZ
        way = 0 if sign > 0 else 1
        if t == 0:
            src = panel.at[k, d]
        else:
            a_copies[k, sign, t - 1].wait_recv()
            src = land_a.at[k, way, t - 1]
            src[...] += panel[k, d]
        a_copies[k, sign, t] = send(src, land_a.at[k, way, t], at_z(sign))

    small[0].wait()
    for k in range(STEPS):
        loads[k].wait()
        for s in range(MEMBERS):
            standardize(s, k * PANEL, k)
        if k == 0:
            pl.semaphore_wait(barrier, len(peers))
        for sign in (1, -1):
            send_a(k, sign, 0)
    loads[2].wait()
    for t in range(1, 4):
        some_rest(2)
        for k in range(STEPS):
            for sign in (1, -1):
                if t < hops(k, sign):
                    send_a(k, sign, t)
    some_rest(2)

    b_copies = {}
    for k in range(STEPS):
        for sign in (1, -1):
            a_copies[k, sign, hops(k, sign) - 1].wait_recv()
        got = [land_a[k, w, hops(k, sign) - 1] for w, sign in ((0, 1), (1, -1))]
        mid[k] = (panel[k, zi] + got[0] + got[1]).reshape(NY, PIECE, FRAMES)
        for o in (2, 1, 3):
            b_copies[k, o] = send(
                mid.at[k, (yi + o) % NY], land_b.at[k, o - 1], at_y(o)
            )
    g_copies = {}
    for k in range(STEPS):
        for o in range(1, NY):
            b_copies[k, o].wait_recv()
        whole[k, zi, yi] = mid[k, yi] + land_b[k, 0] + land_b[k, 1] + land_b[k, 2]
        for o in (2, 1, 3):
            g_copies[k, o] = send(
                whole.at[k, zi, yi], whole.at[k, zi, yi], at_y(o)
            )
    some_rest(8)

    small[1].wait()
    halves = []
    for s in range(MEMBERS):
        label = labels_ref[grp * MEMBERS + s]
        same = jnp.int32(0)
        for i in range(N_GRP * MEMBERS):
            same += jnp.where(labels_ref[i] == label, 1, 0)
        counted = jnp.full((1, TILE), same.astype(jnp.float32))
        halves.append(0.5 / (COHORTS * counted))

    c_copies, e_copies = {}, {}

    def send_c(k, sign, t):
        d = (zi - sign * t + NZ) % NZ
        c_copies[k, sign, t] = send(whole.at[k, d], whole.at[k, d], at_z(sign))

    def compute(offsets):
        chunks = [(zi + o + NZ) % NZ for o in offsets]

        def tile(j, carry):
            cols = pl.ds(pl.multiple_of(j * TILE, TILE), TILE)
            total = None
            for s in range(MEMBERS):
                rows = jnp.concatenate(
                    [
                        whole[k, d, pl.ds(s * NC, NC)].reshape(SHARE, FRAMES)
                        for d in chunks
                        for k in range(STEPS)
                    ],
                    axis=0,
                )
                q = jnp.dot(
                    rows, scored[s, :, cols], preferred_element_type=jnp.float32
                ) * (1.0 / FRAMES)
                q = jnp.clip(q, -clip_limit, clip_limit)
                term = halves[s] * jnp.log((1.0 + q) / (1.0 - q))
                total = term if total is None else total + term
            total = total.astype(jnp.bfloat16).reshape(
                len(chunks), STEPS, NC, OUT_ROWS, TILE
            )
            for i, d in enumerate(chunks):
                part[d, :, :, :, cols] = total[i]
            return carry

        lax.fori_loop(0, COLUMNS // TILE, tile, 0)
        for o, d in zip(offsets, chunks):
            e_copies[o] = send(part.at[d, :, 1 - core], land_e.at[d], other_core)

    base = count[0]
    count[0] += NQ - 1

    def h_copy(o, d):
        k = base + o - 1
        return pltpu.make_async_remote_copy(
            src_ref=half.at[d],
            dst_ref=land_h.at[o - 1],
            send_sem=send_sem.at[k],
            recv_sem=recv_sem.at[k],
            device_id={"grp": d * NC + core},
            device_id_type=MESH,
        )

    def forward(offsets):
        for o in offsets:
            d = (zi + o + NZ) % NZ
            e_copies[o].wait_recv()
            half[d] = (
                part[d, :, core].astype(jnp.float32) + land_e[d].astype(jnp.float32)
            ).astype(jnp.bfloat16)
            away = (d - qi + NQ) % NQ

            @pl.when(away != 0)
            def _():
                h_copy(away, d).start()

    for k in range(STEPS):
        for o in range(1, NY):
            g_copies[k, o].wait_recv()
        for sign in (1, -1):
            send_c(k, sign, 0)
    groups = [(0,), (1, -1), (2, -2), (3, -3), (4,)]
    compute(groups[0])
    for t in range(4):
        for k in range(STEPS):
            for sign in (1, -1):
                if t < hops(k, sign):
                    c_copies[k, sign, t].wait_recv()
                if t + 1 < hops(k, sign):
                    send_c(k, sign, t + 1)
        forward(groups[t])
        compute(groups[t + 1])
    forward(groups[4])

    total = half[qi].astype(jnp.float32)
    for o in range(1, NQ):
        h_copy(o, (qi + o) % NQ).wait_recv()
        total += land_h[o - 1].astype(jnp.float32)
    for k in range(STEPS):
        upper = blk >= owner_ref[k]
        out_ref[k] = jnp.where(upper, total[k], 0.0).astype(out_ref.dtype)

    for copies in (a_copies, b_copies, g_copies, c_copies, e_copies):
        for copy in copies.values():
            copy.wait_send()
    for o in range(1, NQ):
        h_copy(o, (qi + o) % NQ).wait_send()


def body(series, labels, panel_owner):
    half_type = jnp.bfloat16
    return pl.pallas_call(
        kernel,
        out_shape=jax.ShapeDtypeStruct((STEPS, OUT_ROWS, COLUMNS), half_type),
        in_specs=[pl.BlockSpec(memory_space=pltpu.HBM)] * 3,
        out_specs=pl.BlockSpec(memory_space=pltpu.VMEM),
        scratch_shapes=[
            pltpu.SMEM((N_GRP * MEMBERS,), jnp.int32),
            pltpu.SMEM((STEPS,), jnp.int32),
            pltpu.VMEM((MEMBERS, FRAMES, COLUMNS), half_type),
            pltpu.VMEM((MEMBERS, FRAMES, COLUMNS), half_type),
            pltpu.VMEM((STEPS, NZ, CHUNK, FRAMES), half_type),
            pltpu.VMEM((STEPS, 2, 4, CHUNK, FRAMES), half_type),
            pltpu.VMEM((STEPS, NY, PIECE, FRAMES), half_type),
            pltpu.VMEM((STEPS, NY - 1, PIECE, FRAMES), half_type),
            pltpu.VMEM((STEPS, NZ, NY, PIECE, FRAMES), half_type),
            pltpu.VMEM((NQ, STEPS, NC, OUT_ROWS, COLUMNS), half_type),
            pltpu.VMEM((NQ, STEPS, OUT_ROWS, COLUMNS), half_type),
            pltpu.VMEM((NQ, STEPS, OUT_ROWS, COLUMNS), half_type),
            pltpu.VMEM((NQ - 1, STEPS, OUT_ROWS, COLUMNS), half_type),
            pltpu.SemaphoreType.DMA((5,)),
            pltpu.SemaphoreType.DMA((N_COPIES,)),
            pltpu.SemaphoreType.DMA((N_COPIES,)),
        ],
        compiler_params=pltpu.CompilerParams(
            collective_id=0, has_side_effects=True, vmem_limit_bytes=60 * 1024 * 1024
        ),
    )(labels, panel_owner, series)


def solution(mesh):
    in_specs = (P("grp", None, "blk"), P(), P())
    out_specs = P(None, "grp", "blk")
    return jax.shard_map(body, mesh=mesh, in_specs=in_specs, out_specs=out_specs, check_vma=False)
```

```python
import functools

import jax
import jax.numpy as jnp
from jax import lax
from jax.experimental import pallas as pl
from jax.experimental.pallas import tpu as pltpu
from jax.sharding import PartitionSpec as P

MESH = pl.DeviceIdType.MESH
STEPS, PANEL, COHORTS, MEMBERS = 2, 256, 4, 2
FRAMES, COLUMNS = 512, 1536
NZ, NY, NQ, NC = 8, 4, 8, 2
N_GRP, N_BLK = NQ * NC, NZ * NY
CHUNK = MEMBERS * PANEL // NZ
PIECE = CHUNK // NY
SHARE = PANEL // NZ
OUT_ROWS = PANEL // N_GRP
TILE = 256
ROWS = 128
epsilon = 1e-05
clip_limit = 0.99

N_COPIES = STEPS * (7 + 7) + 6 + NQ + NQ - 1


def kernel(
    labels_hbm, owner_hbm, series_ref, out_ref,
    labels_ref, owner_ref, raw, scored, panel, land_a, mid, land_b, whole,
    part, land_e, half, land_h, load_sem, send_sem, recv_sem,
):
    grp, blk = lax.axis_index("grp"), lax.axis_index("blk")
    zi, yi = blk // NY, blk % NY
    qi, core = grp // NC, grp % NC

    def at_z(offset):
        return {"blk": ((zi + offset + NZ) % NZ) * NY + yi}

    def at_y(offset):
        return {"blk": zi * NY + (yi + offset) % NY}

    def at_q(offset):
        return {"grp": ((qi + offset) % NQ) * NC + core}

    other_core = {"grp": qi * NC + 1 - core}

    loads = []
    small = [
        pltpu.make_async_copy(owner_hbm, owner_ref, load_sem.at[3]),
        pltpu.make_async_copy(labels_hbm, labels_ref, load_sem.at[4]),
    ]
    for copy in small:
        copy.start()
    for k, (start, width) in enumerate(
        [(0, PANEL), (PANEL, PANEL), (STEPS * PANEL, COLUMNS - STEPS * PANEL)]
    ):
        window = (slice(None), slice(None), pl.ds(start, width))
        loads.append(
            pltpu.make_async_copy(series_ref.at[window], raw.at[window], load_sem.at[k])
        )
        loads[-1].start()

    barrier = pltpu.get_barrier_semaphore()
    peers = [at_z(o) for o in (1, -1, 2, -2)]
    peers += [at_y(o) for o in range(1, NY)]
    peers += [other_core]
    peers += [at_q(o) for o in range(1, NQ)]
    for peer in peers:
        pl.semaphore_signal(barrier, inc=1, device_id=peer, device_id_type=MESH)

    count = [0]

    def send(src, dst, device):
        k = count[0]
        count[0] += 1
        copy = pltpu.make_async_remote_copy(
            src_ref=src,
            dst_ref=dst,
            send_sem=send_sem.at[k],
            recv_sem=recv_sem.at[k],
            device_id=device,
            device_id_type=MESH,
        )
        copy.start()
        return copy

    def standardize(s, start, step):
        cols = pl.ds(start, TILE)
        total = jnp.zeros((8, TILE), jnp.float32)
        for r in range(0, FRAMES, ROWS):
            x = raw[s, pl.ds(r, ROWS), cols].astype(jnp.float32)
            total += jnp.sum(x.reshape(ROWS // 8, 8, TILE), axis=0)
        center = jnp.sum(total, axis=0, keepdims=True) * (1.0 / FRAMES)
        total = jnp.zeros((8, TILE), jnp.float32)
        for r in range(0, FRAMES, ROWS):
            x = raw[s, pl.ds(r, ROWS), cols].astype(jnp.float32) - center
            total += jnp.sum((x * x).reshape(ROWS // 8, 8, TILE), axis=0)
        spread = jnp.sum(total, axis=0, keepdims=True) * (1.0 / FRAMES)
        scale = lax.rsqrt(spread + epsilon)
        for r in range(0, FRAMES, ROWS):
            x = raw[s, pl.ds(r, ROWS), cols].astype(jnp.float32) - center
            y = x * scale
            scored[s, pl.ds(r, ROWS), cols] = y.astype(jnp.bfloat16)
            if step is not None:
                mine = jnp.where(owner_ref[step] == blk, 1.0, 0.0)
                turned = (y * mine).T.astype(jnp.bfloat16)
                panel[step, :, pl.ds(s * SHARE, SHARE), pl.ds(r, ROWS)] = turned.reshape(
                    NZ, SHARE, ROWS
                )

    rest = [
        (s, c) for s in range(MEMBERS) for c in range(STEPS * PANEL, COLUMNS, TILE)
    ]

    def some_rest(n):
        for _ in range(n):
            if rest:
                standardize(*rest.pop(0), None)

    def far(k, sign):
        return (sign > 0) == (k == 0)

    a_copies = {}

    def send_a(k, sign, t):
        way = 0 if sign > 0 else 1
        d = (zi + sign * (3 - t) + NZ) % NZ
        if t == 0:
            if far(k, sign):
                a_copies[k, sign, 3] = send(
                    panel.at[k, (zi + 4) % NZ], land_a.at[k, way, 3], at_z(2 * sign)
                )
            src = panel.at[k, d]
        else:
            a_copies[k, sign, t - 1].wait_recv()
            src = land_a.at[k, way, t - 1]
            if t == 1 and far(k, sign):
                a_copies[k, sign, 3].wait_recv()
                src[...] += panel[k, d] + land_a[k, way, 3]
            else:
                src[...] += panel[k, d]
        a_copies[k, sign, t] = send(src, land_a.at[k, way, t], at_z(sign))

    small[0].wait()
    for k in range(STEPS):
        loads[k].wait()
        for s in range(MEMBERS):
            standardize(s, k * PANEL, k)
        if k == 0:
            pl.semaphore_wait(barrier, len(peers))
        for sign in (1, -1):
            send_a(k, sign, 0)
    loads[2].wait()
    for t in range(1, 3):
        some_rest(3)
        for k in range(STEPS):
            for sign in (1, -1):
                send_a(k, sign, t)
    some_rest(2)

    for k in range(STEPS):
        for sign in (1, -1):
            a_copies[k, sign, 2].wait_recv()
        mid[:, k] = (panel[k, zi] + land_a[k, 0, 2] + land_a[k, 1, 2]).reshape(
            NY, PIECE, FRAMES
        )
    b_copies = {}
    for o in (2, 1, 3):
        b_copies[o] = send(mid.at[(yi + o) % NY], land_b.at[o - 1], at_y(o))
    for o in range(1, NY):
        b_copies[o].wait_recv()
    whole[zi, yi] = mid[yi] + land_b[0] + land_b[1] + land_b[2]
    g_copies = {}
    for o in (2, 1, 3):
        g_copies[o] = send(whole.at[zi, yi], whole.at[zi, yi], at_y(o))

    small[1].wait()
    halves = []
    for s in range(MEMBERS):
        label = labels_ref[grp * MEMBERS + s]
        same = jnp.int32(0)
        for i in range(N_GRP * MEMBERS):
            same += jnp.where(labels_ref[i] == label, 1, 0)
        counted = jnp.full((1, TILE), same.astype(jnp.float32))
        halves.append(0.5 / (COHORTS * counted))

    c_copies, e_copies = {}, {}

    def send_c(k, sign, t):
        d = (zi - sign * t + NZ) % NZ
        chunk = whole.at[d, :, k]
        if t == 2 and far(k, sign):
            c_copies[k, sign, 3] = send(chunk, chunk, at_z(2 * sign))
        c_copies[k, sign, t] = send(chunk, chunk, at_z(sign))

    def compute(offsets):
        chunks = [(zi + o + NZ) % NZ for o in offsets]

        def tile(j, carry):
            cols = pl.ds(pl.multiple_of(j * TILE, TILE), TILE)
            total = None
            for s in range(MEMBERS):
                rows = jnp.concatenate(
                    [
                        whole[d, pl.ds(s * NC, NC)].reshape(STEPS * SHARE, FRAMES)
                        for d in chunks
                    ],
                    axis=0,
                )
                q = jnp.dot(
                    rows, scored[s, :, cols], preferred_element_type=jnp.float32
                ) * (1.0 / FRAMES)
                q = jnp.clip(q, -clip_limit, clip_limit)
                term = halves[s] * jnp.log((1.0 + q) / (1.0 - q))
                total = term if total is None else total + term
            total = total.astype(jnp.bfloat16).reshape(
                len(chunks), NC, STEPS, OUT_ROWS, TILE
            )
            for i, d in enumerate(chunks):
                part[d, :, :, :, cols] = total[i]
            return carry

        lax.fori_loop(0, COLUMNS // TILE, tile, 0)
        for o, d in zip(offsets, chunks):
            e_copies[o] = send(part.at[d, 1 - core], land_e.at[d], other_core)

    base = count[0]
    count[0] += NQ - 1

    def h_copy(o, d):
        k = base + o - 1
        return pltpu.make_async_remote_copy(
            src_ref=half.at[d],
            dst_ref=land_h.at[o - 1],
            send_sem=send_sem.at[k],
            recv_sem=recv_sem.at[k],
            device_id={"grp": d * NC + core},
            device_id_type=MESH,
        )

    def forward(offsets):
        for o in offsets:
            d = (zi + o + NZ) % NZ
            e_copies[o].wait_recv()
            half[d] = (
                part[d, core].astype(jnp.float32) + land_e[d].astype(jnp.float32)
            ).astype(jnp.bfloat16)
            away = (d - qi + NQ) % NQ

            @pl.when(away != 0)
            def _():
                h_copy(away, d).start()

    for o in range(1, NY):
        g_copies[o].wait_recv()
    for k in range(STEPS):
        for sign in (1, -1):
            send_c(k, sign, 0)
    compute((0,))
    for t in range(1, 3):
        for k in range(STEPS):
            for sign in (1, -1):
                c_copies[k, sign, t - 1].wait_recv()
                send_c(k, sign, t)
        forward((0,) if t == 1 else (1, -1))
        compute((t, -t))
    for t in (3, 2):
        for k in range(STEPS):
            for sign in (1, -1):
                if (k, sign, t) in c_copies:
                    c_copies[k, sign, t].wait_recv()
    forward((2, -2))
    compute((3, -3))
    compute((4,))
    forward((3, -3, 4))

    total = half[qi].astype(jnp.float32)
    for o in range(1, NQ):
        h_copy(o, (qi + o) % NQ).wait_recv()
        total += land_h[o - 1].astype(jnp.float32)
    for k in range(STEPS):
        upper = blk >= owner_ref[k]
        out_ref[k] = jnp.where(upper, total[k], 0.0)

    for copies in (a_copies, b_copies, g_copies, c_copies, e_copies):
        for copy in copies.values():
            copy.wait_send()
    for o in range(1, NQ):
        h_copy(o, (qi + o) % NQ).wait_send()


def body(series, labels, panel_owner):
    half_type = jnp.bfloat16
    summed = pl.pallas_call(
        kernel,
        out_shape=jax.ShapeDtypeStruct((STEPS, OUT_ROWS, COLUMNS), jnp.float32),
        in_specs=[pl.BlockSpec(memory_space=pltpu.HBM)] * 3,
        out_specs=pl.BlockSpec(memory_space=pltpu.VMEM),
        scratch_shapes=[
            pltpu.SMEM((N_GRP * MEMBERS,), jnp.int32),
            pltpu.SMEM((STEPS,), jnp.int32),
            pltpu.VMEM((MEMBERS, FRAMES, COLUMNS), half_type),
            pltpu.VMEM((MEMBERS, FRAMES, COLUMNS), half_type),
            pltpu.VMEM((STEPS, NZ, CHUNK, FRAMES), half_type),
            pltpu.VMEM((STEPS, 2, 4, CHUNK, FRAMES), half_type),
            pltpu.VMEM((NY, STEPS, PIECE, FRAMES), half_type),
            pltpu.VMEM((NY - 1, STEPS, PIECE, FRAMES), half_type),
            pltpu.VMEM((NZ, NY, STEPS, PIECE, FRAMES), half_type),
            pltpu.VMEM((NQ, NC, STEPS, OUT_ROWS, COLUMNS), half_type),
            pltpu.VMEM((NQ, STEPS, OUT_ROWS, COLUMNS), half_type),
            pltpu.VMEM((NQ, STEPS, OUT_ROWS, COLUMNS), half_type),
            pltpu.VMEM((NQ - 1, STEPS, OUT_ROWS, COLUMNS), half_type),
            pltpu.SemaphoreType.DMA((5,)),
            pltpu.SemaphoreType.DMA((N_COPIES,)),
            pltpu.SemaphoreType.DMA((N_COPIES,)),
        ],
        compiler_params=pltpu.CompilerParams(
            collective_id=0, has_side_effects=True, vmem_limit_bytes=60 * 1024 * 1024
        ),
    )(labels, panel_owner, series)
    return summed.astype(half_type)


def solution(mesh):
    in_specs = (P("grp", None, "blk"), P(), P())
    out_specs = P(None, "grp", "blk")
    return jax.shard_map(body, mesh=mesh, in_specs=in_specs, out_specs=out_specs, check_vma=False)
```

```python
import functools

import jax
import jax.numpy as jnp
from jax import lax
from jax.experimental import pallas as pl
from jax.experimental.pallas import tpu as pltpu
from jax.sharding import PartitionSpec as P

MESH = pl.DeviceIdType.MESH
STEPS, PANEL, COHORTS, MEMBERS = 2, 256, 4, 2
FRAMES, COLUMNS = 512, 1536
NZ, NY, NQ, NC = 8, 4, 8, 2
N_GRP, N_BLK = NQ * NC, NZ * NY
PIECE = PANEL // NZ
OUT_ROWS = PANEL // N_GRP
TILE = 256
WIDE = 512
ROWS = 128
epsilon = 1e-05
clip_limit = 0.99

N_COPIES = NY * (7 + 7) + 6 + NQ + NQ - 1


def kernel(
    labels_hbm, owner_hbm, series_ref, out_ref,
    labels_ref, owner_ref, raw, scored, panel, land_a, mid, land_b, whole,
    part, land_e, half, land_h, load_sem, send_sem, recv_sem,
):
    grp, blk = lax.axis_index("grp"), lax.axis_index("blk")
    zi, yi = blk // NY, blk % NY
    qi, core = grp // NC, grp % NC

    def at_z(offset):
        return {"blk": ((zi + offset + NZ) % NZ) * NY + yi}

    def at_y(offset):
        return {"blk": zi * NY + (yi + offset) % NY}

    def at_q(offset):
        return {"grp": ((qi + offset) % NQ) * NC + core}

    other_core = {"grp": qi * NC + 1 - core}

    loads = []
    small = [
        pltpu.make_async_copy(owner_hbm, owner_ref, load_sem.at[3]),
        pltpu.make_async_copy(labels_hbm, labels_ref, load_sem.at[4]),
    ]
    for copy in small:
        copy.start()
    for k, (start, width) in enumerate(
        [(0, PANEL), (PANEL, PANEL), (STEPS * PANEL, COLUMNS - STEPS * PANEL)]
    ):
        window = (slice(None), slice(None), pl.ds(start, width))
        loads.append(
            pltpu.make_async_copy(series_ref.at[window], raw.at[window], load_sem.at[k])
        )
        loads[-1].start()

    barrier = pltpu.get_barrier_semaphore()
    peers = [at_y(o) for o in (2, 1, 3)]
    peers += [at_z(o) for o in (1, -1, 2, -2)]
    peers += [at_q(o) for o in range(1, NQ)]
    peers += [other_core]
    for peer in peers:
        pl.semaphore_signal(barrier, inc=1, device_id=peer, device_id_type=MESH)

    count = [0]

    def send(src, dst, device):
        k = count[0]
        count[0] += 1
        copy = pltpu.make_async_remote_copy(
            src_ref=src,
            dst_ref=dst,
            send_sem=send_sem.at[k],
            recv_sem=recv_sem.at[k],
            device_id=device,
            device_id_type=MESH,
        )
        copy.start()
        return copy

    def standardize(s, start, step):
        cols = pl.ds(start, TILE)
        total = jnp.zeros((8, TILE), jnp.float32)
        for r in range(0, FRAMES, ROWS):
            x = raw[s, pl.ds(r, ROWS), cols].astype(jnp.float32)
            total += jnp.sum(x.reshape(ROWS // 8, 8, TILE), axis=0)
        center = jnp.sum(total, axis=0, keepdims=True) * (1.0 / FRAMES)
        total = jnp.zeros((8, TILE), jnp.float32)
        for r in range(0, FRAMES, ROWS):
            x = raw[s, pl.ds(r, ROWS), cols].astype(jnp.float32) - center
            total += jnp.sum((x * x).reshape(ROWS // 8, 8, TILE), axis=0)
        spread = jnp.sum(total, axis=0, keepdims=True) * (1.0 / FRAMES)
        scale = lax.rsqrt(spread + epsilon)
        for r in range(0, FRAMES, ROWS):
            x = raw[s, pl.ds(r, ROWS), cols].astype(jnp.float32) - center
            y = x * scale
            scored[s, pl.ds(r, ROWS), cols] = y.astype(jnp.bfloat16)
            if step is not None:
                mine = jnp.where(owner_ref[step] == blk, 1.0, 0.0)
                turned = (y * mine).T.astype(jnp.bfloat16)
                panel[:, s * STEPS + step, :, pl.ds(r, ROWS)] = turned.reshape(
                    NZ, PIECE, ROWS
                )

    rest = [
        (s, c) for s in range(MEMBERS) for c in range(STEPS * PANEL, COLUMNS, TILE)
    ]

    def some_rest(n):
        for _ in range(n):
            if rest:
                standardize(*rest.pop(0), None)

    def far(o, sign):
        return (sign > 0) == (o % 2 == 0)

    SIGNS = (1, -1)
    a_copies = {}

    def send_a(o, sign, t):
        way = 0 if sign > 0 else 1
        j = (yi + o) % NY
        mine = panel.at[(zi + sign * (3 - t) + NZ) % NZ, j]
        if t == 0:
            if far(o, sign):
                a_copies[o, sign, 3] = send(
                    panel.at[(zi + 4) % NZ, j], land_a.at[o, way, 3], at_z(2 * sign)
                )
            src = mine
        else:
            a_copies[o, sign, t - 1].wait_recv()
            src = land_a.at[o, way, t - 1]
            if t == 1 and far(o, sign):
                a_copies[o, sign, 3].wait_recv()
                src[...] += mine[...] + land_a[o, way, 3]
            else:
                src[...] += mine[...]
        a_copies[o, sign, t] = send(src, land_a.at[o, way, t], at_z(sign))

    small[0].wait()
    for k in range(STEPS):
        loads[k].wait()
        for s in range(MEMBERS):
            standardize(s, k * PANEL, k)
    pl.semaphore_wait(barrier, len(peers))
    order = (2, 1, 3, 0)
    for o in order:
        for sign in SIGNS:
            send_a(o, sign, 0)
    loads[2].wait()
    some_rest(4)
    for t in range(1, 3):
        for o in order:
            for sign in SIGNS:
                send_a(o, sign, t)
        some_rest(2)

    b_copies = {}
    for o in order:
        for sign in SIGNS:
            a_copies[o, sign, 2].wait_recv()
        mid[o] = panel[zi, (yi + o) % NY] + land_a[o, 0, 2] + land_a[o, 1, 2]
        if o:
            b_copies[o] = send(mid.at[o], land_b.at[o - 1], at_y(o))
    for o in (1, 3, 2):
        b_copies[o].wait_recv()
    whole[zi, yi] = mid[0] + land_b[0] + land_b[1] + land_b[2]
    g_copies, c_copies = {}, {}

    def send_c(o, sign, t):
        if t:
            c_copies[o, sign, t - 1].wait_recv()
        piece = whole.at[(zi - sign * t + NZ) % NZ, (yi - o + NY) % NY]
        if t == 2 and far(o, sign):
            c_copies[o, sign, 3] = send(piece, piece, at_z(2 * sign))
        c_copies[o, sign, t] = send(piece, piece, at_z(sign))

    for o in (2, 1, 3):
        g_copies[o] = send(whole.at[zi, yi], whole.at[zi, yi], at_y(o))
    for sign in SIGNS:
        send_c(0, sign, 0)

    small[1].wait()
    halves = []
    for s in range(MEMBERS):
        label = labels_ref[grp * MEMBERS + s]
        same = jnp.int32(0)
        for i in range(N_GRP * MEMBERS):
            same += jnp.where(labels_ref[i] == label, 1, 0)
        counted = jnp.full((1, WIDE), same.astype(jnp.float32))
        halves.append(0.5 / (COHORTS * counted))

    e_copies = {}

    def compute(offsets):
        chunks = [(zi + o + NZ) % NZ for o in offsets]

        def tile(j, carry):
            cols = pl.ds(pl.multiple_of(j * WIDE, WIDE), WIDE)
            total = None
            for s in range(MEMBERS):
                rows = jnp.concatenate(
                    [
                        whole[d, pl.ds(s * STEPS, STEPS)].reshape(STEPS * PIECE, FRAMES)
                        for d in chunks
                    ],
                    axis=0,
                )
                q = jnp.dot(
                    rows, scored[s, :, cols], preferred_element_type=jnp.float32
                ) * (1.0 / FRAMES)
                q = jnp.clip(q, -clip_limit, clip_limit)
                term = halves[s] * (jnp.log(1.0 + q) - jnp.log(1.0 - q))
                total = term if total is None else total + term
            total = total.astype(jnp.bfloat16).reshape(
                len(chunks), STEPS, NC, OUT_ROWS, WIDE
            )
            for i, d in enumerate(chunks):
                for k in range(STEPS):
                    for c in range(NC):
                        part[d, c, k, :, cols] = total[i, k, c]
            return carry

        lax.fori_loop(0, COLUMNS // WIDE, tile, 0)
        for o, d in zip(offsets, chunks):
            e_copies[o] = send(part.at[d, 1 - core], land_e.at[d], other_core)

    base = count[0]
    count[0] += NQ - 1

    def h_copy(o, d):
        k = base + o - 1
        return pltpu.make_async_remote_copy(
            src_ref=half.at[d],
            dst_ref=land_h.at[o - 1],
            send_sem=send_sem.at[k],
            recv_sem=recv_sem.at[k],
            device_id={"grp": d * NC + core},
            device_id_type=MESH,
        )

    def forward(offsets):
        for o in offsets:
            d = (zi + o + NZ) % NZ
            e_copies[o].wait_recv()
            half[d] = (
                part[d, core].astype(jnp.float32) + land_e[d].astype(jnp.float32)
            ).astype(jnp.bfloat16)
            away = (d - qi + NQ) % NQ

            @pl.when(away != 0)
            def _():
                h_copy(away, d).start()

    def hop(o, t):
        if t == 0:
            g_copies[o].wait_recv()
        for sign in SIGNS:
            send_c(o, sign, t)

    hop(1, 0)
    hop(3, 0)
    hop(0, 1)
    hop(2, 0)
    compute((0,))
    hop(1, 1)
    hop(3, 1)
    hop(0, 2)
    hop(2, 1)
    forward((0,))
    compute((1, -1))
    hop(1, 2)
    hop(3, 2)
    hop(2, 2)
    forward((1, -1))
    compute((2, -2))
    forward((2, -2))
    for o in (0, 1, 3, 2):
        for sign in SIGNS:
            c_copies[o, sign, 2].wait_recv()
    compute((3, -3))
    for o in (0, 1, 3, 2):
        for sign in SIGNS:
            if far(o, sign):
                c_copies[o, sign, 3].wait_recv()
    compute((4,))
    forward((3, -3, 4))

    total = half[qi].astype(jnp.float32)
    for o in range(1, NQ):
        h_copy(o, (qi + o) % NQ).wait_recv()
        total += land_h[o - 1].astype(jnp.float32)
    for k in range(STEPS):
        upper = blk >= owner_ref[k]
        out_ref[k] = jnp.where(upper, total[k], 0.0)

    for copies in (a_copies, b_copies, g_copies, c_copies, e_copies):
        for copy in copies.values():
            copy.wait_send()
    for o in range(1, NQ):
        h_copy(o, (qi + o) % NQ).wait_send()


def body(series, labels, panel_owner):
    half_type = jnp.bfloat16
    summed = pl.pallas_call(
        kernel,
        out_shape=jax.ShapeDtypeStruct((STEPS, OUT_ROWS, COLUMNS), jnp.float32),
        in_specs=[pl.BlockSpec(memory_space=pltpu.HBM)] * 3,
        out_specs=pl.BlockSpec(memory_space=pltpu.VMEM),
        scratch_shapes=[
            pltpu.SMEM((N_GRP * MEMBERS,), jnp.int32),
            pltpu.SMEM((STEPS,), jnp.int32),
            pltpu.VMEM((MEMBERS, FRAMES, COLUMNS), half_type),
            pltpu.VMEM((MEMBERS, FRAMES, COLUMNS), half_type),
            pltpu.VMEM((NZ, NY, PIECE, FRAMES), half_type),
            pltpu.VMEM((NY, 2, 4, PIECE, FRAMES), half_type),
            pltpu.VMEM((NY, PIECE, FRAMES), half_type),
            pltpu.VMEM((NY - 1, PIECE, FRAMES), half_type),
            pltpu.VMEM((NZ, NY, PIECE, FRAMES), half_type),
            pltpu.VMEM((NQ, NC, STEPS, OUT_ROWS, COLUMNS), half_type),
            pltpu.VMEM((NQ, STEPS, OUT_ROWS, COLUMNS), half_type),
            pltpu.VMEM((NQ, STEPS, OUT_ROWS, COLUMNS), half_type),
            pltpu.VMEM((NQ - 1, STEPS, OUT_ROWS, COLUMNS), half_type),
            pltpu.SemaphoreType.DMA((5,)),
            pltpu.SemaphoreType.DMA((N_COPIES,)),
            pltpu.SemaphoreType.DMA((N_COPIES,)),
        ],
        compiler_params=pltpu.CompilerParams(
            collective_id=0, has_side_effects=True, vmem_limit_bytes=60 * 1024 * 1024
        ),
    )(labels, panel_owner, series)
    return summed.astype(half_type)


def solution(mesh):
    in_specs = (P("grp", None, "blk"), P(), P())
    out_specs = P(None, "grp", "blk")
    return jax.shard_map(body, mesh=mesh, in_specs=in_specs, out_specs=out_specs, check_vma=False)
```

```python
import functools

import jax
import jax.numpy as jnp
from jax import lax
from jax.experimental import pallas as pl
from jax.experimental.pallas import tpu as pltpu
from jax.sharding import PartitionSpec as P

MESH = pl.DeviceIdType.MESH
STEPS, PANEL, COHORTS, MEMBERS = 2, 256, 4, 2
FRAMES, COLUMNS = 512, 1536
NZ, NY, NQ, NC = 8, 4, 8, 2
N_GRP, N_BLK = NQ * NC, NZ * NY
PIECE = PANEL // NZ
OUT_ROWS = PANEL // N_GRP
TILE = 256
WIDE = 512
ROWS = 128
epsilon = 1e-05
clip_limit = 0.99

N_COPIES = NY * (7 + 7) + 6 + NQ + 3 + STEPS * (NQ - 1)


def kernel(
    labels_hbm, owner_hbm, series_ref, out_ref,
    labels_ref, owner_ref, raw, scored, panel, land_a, mid, land_b, whole,
    part, land_e, half, land_h, load_sem, send_sem, recv_sem,
):
    grp, blk = lax.axis_index("grp"), lax.axis_index("blk")
    zi, yi = blk // NY, blk % NY
    qi, core = grp // NC, grp % NC

    def at_z(offset):
        return {"blk": ((zi + offset + NZ) % NZ) * NY + yi}

    def at_y(offset):
        return {"blk": zi * NY + (yi + offset) % NY}

    def at_q(offset):
        return {"grp": ((qi + offset) % NQ) * NC + core}

    other_core = {"grp": qi * NC + 1 - core}

    loads = []
    small = [
        pltpu.make_async_copy(owner_hbm, owner_ref, load_sem.at[NY + 1]),
        pltpu.make_async_copy(labels_hbm, labels_ref, load_sem.at[NY + 2]),
    ]
    for copy in small:
        copy.start()
    order = (2, 1, 3, 0)
    for i, o in enumerate(order):
        s, k = (yi + o) % NY // STEPS, (yi + o) % STEPS
        cols = pl.ds(pl.multiple_of(k * PANEL, PANEL), PANEL)
        loads.append(
            pltpu.make_async_copy(
                series_ref.at[s, :, cols], raw.at[s, :, cols], load_sem.at[i]
            )
        )
        loads[-1].start()
    cols = pl.ds(STEPS * PANEL, COLUMNS - STEPS * PANEL)
    loads.append(
        pltpu.make_async_copy(
            series_ref.at[:, :, cols], raw.at[:, :, cols], load_sem.at[NY]
        )
    )
    loads[-1].start()

    barrier = pltpu.get_barrier_semaphore()
    peers = [at_y(o) for o in (2, 1, 3)]
    peers += [at_z(o) for o in (1, -1, 2, -2)]
    peers += [at_q(o) for o in range(1, NQ)]
    peers += [other_core]
    for peer in peers:
        pl.semaphore_signal(barrier, inc=1, device_id=peer, device_id_type=MESH)

    count = [0]

    def send(src, dst, device):
        k = count[0]
        count[0] += 1
        copy = pltpu.make_async_remote_copy(
            src_ref=src,
            dst_ref=dst,
            send_sem=send_sem.at[k],
            recv_sem=recv_sem.at[k],
            device_id=device,
            device_id_type=MESH,
        )
        copy.start()
        return copy

    def standardize(s, start, step):
        cols = pl.ds(pl.multiple_of(start, TILE), TILE)
        total = jnp.zeros((8, TILE), jnp.float32)
        for r in range(0, FRAMES, ROWS):
            x = raw[s, pl.ds(r, ROWS), cols].astype(jnp.float32)
            total += jnp.sum(x.reshape(ROWS // 8, 8, TILE), axis=0)
        center = jnp.sum(total, axis=0, keepdims=True) * (1.0 / FRAMES)
        total = jnp.zeros((8, TILE), jnp.float32)
        for r in range(0, FRAMES, ROWS):
            x = raw[s, pl.ds(r, ROWS), cols].astype(jnp.float32) - center
            total += jnp.sum((x * x).reshape(ROWS // 8, 8, TILE), axis=0)
        spread = jnp.sum(total, axis=0, keepdims=True) * (1.0 / FRAMES)
        scale = lax.rsqrt(spread + epsilon)
        for r in range(0, FRAMES, ROWS):
            x = raw[s, pl.ds(r, ROWS), cols].astype(jnp.float32) - center
            y = x * scale
            scored[s, pl.ds(r, ROWS), cols] = y.astype(jnp.bfloat16)
            if step is not None:
                mine = jnp.where(owner_ref[step] == blk, 1.0, 0.0)
                turned = (y * mine).T.astype(jnp.bfloat16)
                turned = turned.reshape(2, NZ // 2, PIECE, ROWS)
                for i in range(2):
                    at = NZ // 2 * (i + step - 2 * i * step)
                    panel[
                        pl.ds(at, NZ // 2), s * STEPS + step, :, pl.ds(r, ROWS)
                    ] = turned[i]

    rest = [
        (s, c) for s in range(MEMBERS) for c in range(STEPS * PANEL, COLUMNS, TILE)
    ]

    def some_rest(n):
        for _ in range(n):
            if rest:
                standardize(*rest.pop(0), None)

    def far(o, sign):
        return (sign > 0) == (o % 2 == 0)

    SIGNS = (1, -1)
    a_copies = {}

    def send_a(o, sign, t):
        way = 0 if sign > 0 else 1
        j = (yi + o) % NY
        mine = panel.at[(zi + sign * (3 - t) + NZ) % NZ, j]
        if t == 0:
            if far(o, sign):
                a_copies[o, sign, 3] = send(
                    panel.at[(zi + 4) % NZ, j], land_a.at[o, way, 3], at_z(2 * sign)
                )
            src = mine
        else:
            a_copies[o, sign, t - 1].wait_recv()
            src = land_a.at[o, way, t - 1]
            if t == 1 and far(o, sign):
                a_copies[o, sign, 3].wait_recv()
                src[...] += mine[...] + land_a[o, way, 3]
            else:
                src[...] += mine[...]
        a_copies[o, sign, t] = send(src, land_a.at[o, way, t], at_z(sign))

    small[0].wait()
    for i, o in enumerate(order):
        loads[i].wait()
        s, k = (yi + o) % NY // STEPS, (yi + o) % STEPS
        standardize(s, k * PANEL, k)
        if i == 0:
            pl.semaphore_wait(barrier, len(peers))
        for sign in SIGNS:
            send_a(o, sign, 0)
    loads[NY].wait()
    some_rest(4)
    for t in range(1, 3):
        for o in order:
            for sign in SIGNS:
                send_a(o, sign, t)
        some_rest(2)

    b_copies = {}
    for o in order:
        for sign in SIGNS:
            a_copies[o, sign, 2].wait_recv()
        mid[o] = panel[zi, (yi + o) % NY] + land_a[o, 0, 2] + land_a[o, 1, 2]
        if o:
            b_copies[o] = send(mid.at[o], land_b.at[o - 1], at_y(o))
    for o in (1, 3, 2):
        b_copies[o].wait_recv()
    whole[zi, yi] = mid[0] + land_b[0] + land_b[1] + land_b[2]
    g_copies, c_copies = {}, {}

    def send_c(o, sign, t):
        if t:
            c_copies[o, sign, t - 1].wait_recv()
        piece = whole.at[(zi - sign * t + NZ) % NZ, (yi - o + NY) % NY]
        if t == 2 and far(o, sign):
            c_copies[o, sign, 3] = send(piece, piece, at_z(2 * sign))
        c_copies[o, sign, t] = send(piece, piece, at_z(sign))

    for o in (2, 1, 3):
        g_copies[o] = send(whole.at[zi, yi], whole.at[zi, yi], at_y(o))
    for sign in SIGNS:
        send_c(0, sign, 0)

    small[1].wait()
    halves = []
    for s in range(MEMBERS):
        label = labels_ref[grp * MEMBERS + s]
        same = jnp.int32(0)
        for i in range(N_GRP * MEMBERS):
            same += jnp.where(labels_ref[i] == label, 1, 0)
        counted = jnp.full((1, WIDE), same.astype(jnp.float32))
        halves.append(0.5 / (COHORTS * counted))

    def compute(offsets, step=None):
        chunks = [(zi + o + NZ) % NZ for o in offsets]
        first, steps = (0, STEPS) if step is None else (step, 1)

        def tile(j, carry):
            cols = pl.ds(pl.multiple_of(j * WIDE, WIDE), WIDE)
            total = None
            for s in range(MEMBERS):
                rows = jnp.concatenate(
                    [
                        whole[d, pl.ds(s * STEPS + first, steps)].reshape(
                            steps * PIECE, FRAMES
                        )
                        for d in chunks
                    ],
                    axis=0,
                )
                q = jnp.dot(
                    rows, scored[s, :, cols], preferred_element_type=jnp.float32
                ) * (1.0 / FRAMES)
                q = jnp.clip(q, -clip_limit, clip_limit)
                term = halves[s] * (jnp.log(1.0 + q) - jnp.log(1.0 - q))
                total = term if total is None else total + term
            total = total.astype(jnp.bfloat16).reshape(
                len(chunks), steps, NC, OUT_ROWS, WIDE
            )
            for i, d in enumerate(chunks):
                for k in range(steps):
                    for c in range(NC):
                        part[d, c, first + k, :, cols] = total[i, k, c]
            return carry

        lax.fori_loop(0, COLUMNS // WIDE, tile, 0)
        mine = pl.ds(first, steps)
        return [
            send(part.at[d, 1 - core, mine], land_e.at[d, mine], other_core)
            for d in chunks
        ]

    base = count[0]
    count[0] += STEPS * (NQ - 1)

    def h_copy(away, d, k):
        at = base + (away - 1) * STEPS + k
        return pltpu.make_async_remote_copy(
            src_ref=half.at[d, k],
            dst_ref=land_h.at[away - 1, k],
            send_sem=send_sem.at[at],
            recv_sem=recv_sem.at[at],
            device_id=at_q(away),
            device_id_type=MESH,
        )

    def forward(offsets, copies, steps=range(STEPS)):
        for o, copy in zip(offsets, copies):
            d = (zi + o + NZ) % NZ
            copy.wait_recv()
            for k in steps:
                half[d, k] = (
                    part[d, core, k].astype(jnp.float32)
                    + land_e[d, k].astype(jnp.float32)
                ).astype(jnp.bfloat16)
                away = (d + NQ // 2 * k - qi + NQ) % NQ

                @pl.when(away != 0)
                def _():
                    h_copy(away, d, k).start()

    def hop(o, t):
        if t == 0:
            g_copies[o].wait_recv()
        for sign in SIGNS:
            send_c(o, sign, t)

    hop(1, 0)
    hop(3, 0)
    hop(0, 1)
    hop(2, 0)
    near = compute((0,))
    hop(1, 1)
    hop(3, 1)
    hop(0, 2)
    hop(2, 1)
    forward((0,), near)
    next_one = compute((1, -1))
    hop(1, 2)
    hop(3, 2)
    hop(2, 2)
    forward((1, -1), next_one)
    next_two = compute((2, -2))
    forward((2, -2), next_two)
    last = []
    for pair in ((1, 3), (0, 2)):
        for o in pair:
            for sign in SIGNS:
                c_copies[o, sign, 2].wait_recv()
                if far(o, sign):
                    c_copies[o, sign, 3].wait_recv()
        k = (yi + pair[0]) % STEPS
        last.append((k, compute((3, -3, 4), k)))
    for k, copies in last:
        forward((3, -3, 4), copies, (k,))

    for k in range(STEPS):
        total = half[(qi + NQ // 2 * k) % NQ, k].astype(jnp.float32)
        for away in range(1, NQ):
            h_copy(away, 0, k).wait_recv()
            total += land_h[away - 1, k].astype(jnp.float32)
        upper = blk >= owner_ref[k]
        out_ref[k] = jnp.where(upper, total, 0.0)

    for copy in near + next_one + next_two + last[0][1] + last[1][1]:
        copy.wait_send()
    for away in range(1, NQ):
        for k in range(STEPS):
            h_copy(away, 0, k).wait_send()
    for copies in (a_copies, b_copies, g_copies, c_copies):
        for copy in copies.values():
            copy.wait_send()


def body(series, labels, panel_owner):
    half_type = jnp.bfloat16
    summed = pl.pallas_call(
        kernel,
        out_shape=jax.ShapeDtypeStruct((STEPS, OUT_ROWS, COLUMNS), jnp.float32),
        in_specs=[pl.BlockSpec(memory_space=pltpu.HBM)] * 3,
        out_specs=pl.BlockSpec(memory_space=pltpu.VMEM),
        scratch_shapes=[
            pltpu.SMEM((N_GRP * MEMBERS,), jnp.int32),
            pltpu.SMEM((STEPS,), jnp.int32),
            pltpu.VMEM((MEMBERS, FRAMES, COLUMNS), half_type),
            pltpu.VMEM((MEMBERS, FRAMES, COLUMNS), half_type),
            pltpu.VMEM((NZ, NY, PIECE, FRAMES), half_type),
            pltpu.VMEM((NY, 2, 4, PIECE, FRAMES), half_type),
            pltpu.VMEM((NY, PIECE, FRAMES), half_type),
            pltpu.VMEM((NY - 1, PIECE, FRAMES), half_type),
            pltpu.VMEM((NZ, NY, PIECE, FRAMES), half_type),
            pltpu.VMEM((NQ, NC, STEPS, OUT_ROWS, COLUMNS), half_type),
            pltpu.VMEM((NQ, STEPS, OUT_ROWS, COLUMNS), half_type),
            pltpu.VMEM((NQ, STEPS, OUT_ROWS, COLUMNS), half_type),
            pltpu.VMEM((NQ - 1, STEPS, OUT_ROWS, COLUMNS), half_type),
            pltpu.SemaphoreType.DMA((NY + 3,)),
            pltpu.SemaphoreType.DMA((N_COPIES,)),
            pltpu.SemaphoreType.DMA((N_COPIES,)),
        ],
        compiler_params=pltpu.CompilerParams(
            collective_id=0, has_side_effects=True, vmem_limit_bytes=60 * 1024 * 1024
        ),
    )(labels, panel_owner, series)
    return summed.astype(half_type)


def solution(mesh):
    in_specs = (P("grp", None, "blk"), P(), P())
    out_specs = P(None, "grp", "blk")
    return jax.shard_map(body, mesh=mesh, in_specs=in_specs, out_specs=out_specs, check_vma=False)
```

```python
import functools

import jax
import jax.numpy as jnp
from jax import lax
from jax.experimental import pallas as pl
from jax.experimental.pallas import tpu as pltpu
from jax.sharding import PartitionSpec as P

MESH = pl.DeviceIdType.MESH
STEPS, PANEL, COHORTS, MEMBERS = 2, 256, 4, 2
FRAMES, COLUMNS = 512, 1536
NZ, NY, NQ, NC = 8, 4, 8, 2
N_GRP, N_BLK = NQ * NC, NZ * NY
PIECE = PANEL // NZ
OUT_ROWS = PANEL // N_GRP
TILE = 256
WIDE = 512
ROWS = 128
epsilon = 1e-05
clip_limit = 0.99

N_COPIES = NY * (7 + 7) + 6 + NQ + 3 + STEPS * (NQ - 1)


def kernel(
    labels_hbm, owner_hbm, series_ref, out_ref,
    labels_ref, owner_ref, raw, scored, panel, land_a, mid, land_b, whole,
    part, land_e, half, land_h, load_sem, send_sem, recv_sem,
):
    grp, blk = lax.axis_index("grp"), lax.axis_index("blk")
    zi, yi = blk // NY, blk % NY
    qi, core = grp // NC, grp % NC

    def at_z(offset):
        return {"blk": ((zi + offset + NZ) % NZ) * NY + yi}

    def at_y(offset):
        return {"blk": zi * NY + (yi + offset) % NY}

    def at_q(offset):
        return {"grp": ((qi + offset) % NQ) * NC + core}

    other_core = {"grp": qi * NC + 1 - core}

    loads = []
    small = [
        pltpu.make_async_copy(owner_hbm, owner_ref, load_sem.at[NY + 1]),
        pltpu.make_async_copy(labels_hbm, labels_ref, load_sem.at[NY + 2]),
    ]
    for copy in small:
        copy.start()
    order = (2, 1, 3, 0)
    for i, o in enumerate(order):
        s, k = (yi + o) % NY // STEPS, (yi + o) % STEPS
        cols = pl.ds(pl.multiple_of(k * PANEL, PANEL), PANEL)
        loads.append(
            pltpu.make_async_copy(
                series_ref.at[s, :, cols], raw.at[s, :, cols], load_sem.at[i]
            )
        )
        loads[-1].start()
    cols = pl.ds(STEPS * PANEL, COLUMNS - STEPS * PANEL)
    loads.append(
        pltpu.make_async_copy(
            series_ref.at[:, :, cols], raw.at[:, :, cols], load_sem.at[NY]
        )
    )
    loads[-1].start()

    barrier = pltpu.get_barrier_semaphore()
    peers = [at_y(o) for o in (2, 1, 3)]
    peers += [at_z(o) for o in (1, -1, 2, -2)]
    peers += [at_q(o) for o in range(1, NQ)]
    peers += [other_core]
    for peer in peers:
        pl.semaphore_signal(barrier, inc=1, device_id=peer, device_id_type=MESH)

    count = [0]

    def send(src, dst, device):
        k = count[0]
        count[0] += 1
        copy = pltpu.make_async_remote_copy(
            src_ref=src,
            dst_ref=dst,
            send_sem=send_sem.at[k],
            recv_sem=recv_sem.at[k],
            device_id=device,
            device_id_type=MESH,
        )
        copy.start()
        return copy

    def standardize(s, start, step):
        cols = pl.ds(pl.multiple_of(start, TILE), TILE)
        total = jnp.zeros((8, TILE), jnp.float32)
        for r in range(0, FRAMES, ROWS):
            x = raw[s, pl.ds(r, ROWS), cols].astype(jnp.float32)
            total += jnp.sum(x.reshape(ROWS // 8, 8, TILE), axis=0)
        center = jnp.sum(total, axis=0, keepdims=True) * (1.0 / FRAMES)
        total = jnp.zeros((8, TILE), jnp.float32)
        for r in range(0, FRAMES, ROWS):
            x = raw[s, pl.ds(r, ROWS), cols].astype(jnp.float32) - center
            total += jnp.sum((x * x).reshape(ROWS // 8, 8, TILE), axis=0)
        spread = jnp.sum(total, axis=0, keepdims=True) * (1.0 / FRAMES)
        scale = lax.rsqrt(spread + epsilon)
        for r in range(0, FRAMES, ROWS):
            x = raw[s, pl.ds(r, ROWS), cols].astype(jnp.float32) - center
            y = x * scale
            scored[s, pl.ds(r, ROWS), cols] = y.astype(jnp.bfloat16)
            if step is not None:
                mine = jnp.where(owner_ref[step] == blk, 1.0, 0.0)
                turned = (y * mine).T.astype(jnp.bfloat16)
                turned = turned.reshape(2, NZ // 2, PIECE, ROWS)
                for i in range(2):
                    at = NZ // 2 * (i + step - 2 * i * step)
                    panel[
                        pl.ds(at, NZ // 2), s * STEPS + step, :, pl.ds(r, ROWS)
                    ] = turned[i]

    rest = [
        (s, c) for s in range(MEMBERS) for c in range(STEPS * PANEL, COLUMNS, TILE)
    ]

    def some_rest(n):
        for _ in range(n):
            if rest:
                standardize(*rest.pop(0), None)

    def far(o, sign):
        return (sign > 0) == (o % 2 == 0)

    SIGNS = (1, -1)
    a_copies = {}

    def side(o, sign, slot):
        return land_a.at[o, 0 if sign > 0 else 1, slot]

    def own(o, offset):
        return panel.at[(zi + offset + NZ) % NZ, (yi + o) % NY]

    def send_outer(o):
        for sign in SIGNS:
            if far(o, sign):
                a_copies[o, sign, 3] = send(
                    own(o, 4), side(o, sign, 3), at_z(2 * sign)
                )
        for sign in SIGNS:
            a_copies[o, sign, 0] = send(
                own(o, 3 * sign), side(o, sign, 0), at_z(sign)
            )

    def send_next(o):
        for sign in SIGNS:
            a_copies[o, sign, 1] = send(own(o, sign), side(o, sign, 1), at_z(sign))

    def send_sum(o):
        for sign in SIGNS:
            a_copies[o, sign, 0].wait_recv()
            src = side(o, sign, 0)
            if far(o, sign):
                a_copies[o, sign, 3].wait_recv()
                src[...] += own(o, 2 * sign)[...] + side(o, sign, 3)[...]
            else:
                src[...] += own(o, 2 * sign)[...]
            a_copies[o, sign, 2] = send(src, side(o, sign, 2), at_z(2 * sign))

    small[0].wait()
    for i, o in enumerate(order):
        loads[i].wait()
        s, k = (yi + o) % NY // STEPS, (yi + o) % STEPS
        standardize(s, k * PANEL, k)
        if i == 0:
            pl.semaphore_wait(barrier, len(peers))
        send_outer(o)
    for o in order:
        send_next(o)
    loads[NY].wait()
    some_rest(4)
    for o in order:
        send_sum(o)
    some_rest(4)

    b_copies = {}
    for o in order:
        total = own(o, 0)[...]
        for sign in SIGNS:
            for slot in (1, 2):
                a_copies[o, sign, slot].wait_recv()
                total += side(o, sign, slot)[...]
        mid[o] = total
        if o:
            b_copies[o] = send(mid.at[o], land_b.at[o - 1], at_y(o))
    for o in (1, 3, 2):
        b_copies[o].wait_recv()
    whole[zi, yi] = mid[0] + land_b[0] + land_b[1] + land_b[2]
    g_copies, c_copies = {}, {}

    def send_c(o, sign, t):
        if t:
            c_copies[o, sign, t - 1].wait_recv()
        piece = whole.at[(zi - sign * t + NZ) % NZ, (yi - o + NY) % NY]
        if t == 2 and far(o, sign):
            c_copies[o, sign, 3] = send(piece, piece, at_z(2 * sign))
        c_copies[o, sign, t] = send(piece, piece, at_z(sign))

    for o in (2, 1, 3):
        g_copies[o] = send(whole.at[zi, yi], whole.at[zi, yi], at_y(o))
    for sign in SIGNS:
        send_c(0, sign, 0)

    small[1].wait()
    halves = []
    for s in range(MEMBERS):
        label = labels_ref[grp * MEMBERS + s]
        same = jnp.int32(0)
        for i in range(N_GRP * MEMBERS):
            same += jnp.where(labels_ref[i] == label, 1, 0)
        counted = jnp.full((1, WIDE), same.astype(jnp.float32))
        halves.append(0.5 / (COHORTS * counted))

    def compute(offsets, step=None):
        chunks = [(zi + o + NZ) % NZ for o in offsets]
        first, steps = (0, STEPS) if step is None else (step, 1)

        def tile(j, carry):
            cols = pl.ds(pl.multiple_of(j * WIDE, WIDE), WIDE)
            total = None
            for s in range(MEMBERS):
                rows = jnp.concatenate(
                    [
                        whole[d, pl.ds(s * STEPS + first, steps)].reshape(
                            steps * PIECE, FRAMES
                        )
                        for d in chunks
                    ],
                    axis=0,
                )
                q = jnp.dot(
                    rows, scored[s, :, cols], preferred_element_type=jnp.float32
                ) * (1.0 / FRAMES)
                q = jnp.clip(q, -clip_limit, clip_limit)
                term = halves[s] * (jnp.log(1.0 + q) - jnp.log(1.0 - q))
                total = term if total is None else total + term
            total = total.astype(jnp.bfloat16).reshape(
                len(chunks), steps, NC, OUT_ROWS, WIDE
            )
            for i, d in enumerate(chunks):
                for k in range(steps):
                    for c in range(NC):
                        part[d, c, first + k, :, cols] = total[i, k, c]
            return carry

        lax.fori_loop(0, COLUMNS // WIDE, tile, 0)
        mine = pl.ds(first, steps)
        return [
            send(part.at[d, 1 - core, mine], land_e.at[d, mine], other_core)
            for d in chunks
        ]

    base = count[0]
    count[0] += STEPS * (NQ - 1)

    def h_copy(away, d, k):
        at = base + (away - 1) * STEPS + k
        return pltpu.make_async_remote_copy(
            src_ref=half.at[d, k],
            dst_ref=land_h.at[away - 1, k],
            send_sem=send_sem.at[at],
            recv_sem=recv_sem.at[at],
            device_id=at_q(away),
            device_id_type=MESH,
        )

    def forward(offsets, copies, steps=range(STEPS)):
        for o, copy in zip(offsets, copies):
            d = (zi + o + NZ) % NZ
            copy.wait_recv()
            for k in steps:
                half[d, k] = (
                    part[d, core, k].astype(jnp.float32)
                    + land_e[d, k].astype(jnp.float32)
                ).astype(jnp.bfloat16)
                away = (d + NQ // 2 * k - qi + NQ) % NQ

                @pl.when(away != 0)
                def _():
                    h_copy(away, d, k).start()

    def hop(t):
        for sign in SIGNS:
            send_c(0, sign, t)

    def spread(o):
        g_copies[o].wait_recv()
        piece = whole.at[zi, (yi - o + NY) % NY]
        for t in (1, 0):
            for sign in SIGNS:
                c_copies[o, sign, t] = send(piece, piece, at_z((t + 1) * sign))

    def spread_on(o):
        for sign in SIGNS:
            c_copies[o, sign, 1].wait_recv()
            piece = whole.at[(zi - 2 * sign + NZ) % NZ, (yi - o + NY) % NY]
            if far(o, sign):
                c_copies[o, sign, 3] = send(piece, piece, at_z(2 * sign))
            c_copies[o, sign, 2] = send(piece, piece, at_z(sign))

    spread(1)
    spread(3)
    hop(1)
    spread(2)
    near = compute((0,))
    hop(2)
    spread_on(1)
    spread_on(3)
    spread_on(2)
    forward((0,), near)
    for o in (1, 3, 2):
        for sign in SIGNS:
            c_copies[o, sign, 0].wait_recv()
    next_one = compute((1, -1))
    next_two = compute((2, -2))
    forward((1, -1), next_one)
    forward((2, -2), next_two)
    last = []
    for pair in ((1, 3), (0, 2)):
        for o in pair:
            for sign in SIGNS:
                c_copies[o, sign, 2].wait_recv()
                if far(o, sign):
                    c_copies[o, sign, 3].wait_recv()
        k = (yi + pair[0]) % STEPS
        last.append((k, compute((3, -3, 4), k)))
    for k, copies in last:
        forward((3, -3, 4), copies, (k,))

    for k in range(STEPS):
        total = half[(qi + NQ // 2 * k) % NQ, k].astype(jnp.float32)
        for away in range(1, NQ):
            h_copy(away, 0, k).wait_recv()
            total += land_h[away - 1, k].astype(jnp.float32)
        upper = blk >= owner_ref[k]
        out_ref[k] = jnp.where(upper, total, 0.0)

    for copy in near + next_one + next_two + last[0][1] + last[1][1]:
        copy.wait_send()
    for away in range(1, NQ):
        for k in range(STEPS):
            h_copy(away, 0, k).wait_send()
    for copies in (a_copies, b_copies, g_copies, c_copies):
        for copy in copies.values():
            copy.wait_send()


def body(series, labels, panel_owner):
    half_type = jnp.bfloat16
    summed = pl.pallas_call(
        kernel,
        out_shape=jax.ShapeDtypeStruct((STEPS, OUT_ROWS, COLUMNS), jnp.float32),
        in_specs=[pl.BlockSpec(memory_space=pltpu.HBM)] * 3,
        out_specs=pl.BlockSpec(memory_space=pltpu.VMEM),
        scratch_shapes=[
            pltpu.SMEM((N_GRP * MEMBERS,), jnp.int32),
            pltpu.SMEM((STEPS,), jnp.int32),
            pltpu.VMEM((MEMBERS, FRAMES, COLUMNS), half_type),
            pltpu.VMEM((MEMBERS, FRAMES, COLUMNS), half_type),
            pltpu.VMEM((NZ, NY, PIECE, FRAMES), half_type),
            pltpu.VMEM((NY, 2, 4, PIECE, FRAMES), half_type),
            pltpu.VMEM((NY, PIECE, FRAMES), half_type),
            pltpu.VMEM((NY - 1, PIECE, FRAMES), half_type),
            pltpu.VMEM((NZ, NY, PIECE, FRAMES), half_type),
            pltpu.VMEM((NQ, NC, STEPS, OUT_ROWS, COLUMNS), half_type),
            pltpu.VMEM((NQ, STEPS, OUT_ROWS, COLUMNS), half_type),
            pltpu.VMEM((NQ, STEPS, OUT_ROWS, COLUMNS), half_type),
            pltpu.VMEM((NQ - 1, STEPS, OUT_ROWS, COLUMNS), half_type),
            pltpu.SemaphoreType.DMA((NY + 3,)),
            pltpu.SemaphoreType.DMA((N_COPIES,)),
            pltpu.SemaphoreType.DMA((N_COPIES,)),
        ],
        compiler_params=pltpu.CompilerParams(
            collective_id=0, has_side_effects=True, vmem_limit_bytes=60 * 1024 * 1024
        ),
    )(labels, panel_owner, series)
    return summed.astype(half_type)


def solution(mesh):
    in_specs = (P("grp", None, "blk"), P(), P())
    out_specs = P(None, "grp", "blk")
    return jax.shard_map(body, mesh=mesh, in_specs=in_specs, out_specs=out_specs, check_vma=False)
```

```python
import functools

import jax
import jax.numpy as jnp
from jax import lax
from jax.experimental import pallas as pl
from jax.experimental.pallas import tpu as pltpu
from jax.sharding import PartitionSpec as P

MESH = pl.DeviceIdType.MESH
STEPS, PANEL, COHORTS, MEMBERS = 2, 256, 4, 2
FRAMES, COLUMNS = 512, 1536
NZ, NY, NQ, NC = 8, 4, 8, 2
N_GRP, N_BLK = NQ * NC, NZ * NY
PIECE = PANEL // NZ
OUT_ROWS = PANEL // N_GRP
TILE = 256
WIDE = 512
ROWS = 128
epsilon = 1e-05
clip_limit = 0.99

N_COPIES = NY * (7 + 7) + 6 + NQ + 3 + STEPS * (NQ - 1)


def kernel(
    labels_hbm, owner_hbm, series_ref, out_ref,
    labels_ref, owner_ref, raw, scored, panel, land_a, mid, land_b, whole,
    part, land_e, half, land_h, load_sem, send_sem, recv_sem,
):
    grp, blk = lax.axis_index("grp"), lax.axis_index("blk")
    zi, yi = blk // NY, blk % NY
    qi, core = grp // NC, grp % NC

    def at_z(offset):
        return {"blk": ((zi + offset + NZ) % NZ) * NY + yi}

    def at_y(offset):
        return {"blk": zi * NY + (yi + offset) % NY}

    def at_q(offset):
        return {"grp": ((qi + offset) % NQ) * NC + core}

    other_core = {"grp": qi * NC + 1 - core}

    loads = []
    small = [
        pltpu.make_async_copy(owner_hbm, owner_ref, load_sem.at[NY + 1]),
        pltpu.make_async_copy(labels_hbm, labels_ref, load_sem.at[NY + 2]),
    ]
    for copy in small:
        copy.start()
    order = (2, 1, 3, 0)
    for i, o in enumerate(order):
        s, k = (yi + o) % NY // STEPS, (yi + o) % STEPS
        cols = pl.ds(pl.multiple_of(k * PANEL, PANEL), PANEL)
        loads.append(
            pltpu.make_async_copy(
                series_ref.at[s, :, cols], raw.at[s, :, cols], load_sem.at[i]
            )
        )
        loads[-1].start()
    cols = pl.ds(STEPS * PANEL, COLUMNS - STEPS * PANEL)
    loads.append(
        pltpu.make_async_copy(
            series_ref.at[:, :, cols], raw.at[:, :, cols], load_sem.at[NY]
        )
    )
    loads[-1].start()

    barrier = pltpu.get_barrier_semaphore()
    peers = [at_y(o) for o in (2, 1, 3)]
    peers += [at_z(o) for o in (1, -1, 2, -2)]
    peers += [at_q(o) for o in range(1, NQ)]
    peers += [other_core]
    for peer in peers:
        pl.semaphore_signal(barrier, inc=1, device_id=peer, device_id_type=MESH)

    count = [0]

    def send(src, dst, device):
        k = count[0]
        count[0] += 1
        copy = pltpu.make_async_remote_copy(
            src_ref=src,
            dst_ref=dst,
            send_sem=send_sem.at[k],
            recv_sem=recv_sem.at[k],
            device_id=device,
            device_id_type=MESH,
        )
        copy.start()
        return copy

    def standardize(s, start, step):
        cols = pl.ds(pl.multiple_of(start, TILE), TILE)
        total = jnp.zeros((8, TILE), jnp.float32)
        for r in range(0, FRAMES, ROWS):
            x = raw[s, pl.ds(r, ROWS), cols].astype(jnp.float32)
            total += jnp.sum(x.reshape(ROWS // 8, 8, TILE), axis=0)
        center = jnp.sum(total, axis=0, keepdims=True) * (1.0 / FRAMES)
        total = jnp.zeros((8, TILE), jnp.float32)
        for r in range(0, FRAMES, ROWS):
            x = raw[s, pl.ds(r, ROWS), cols].astype(jnp.float32) - center
            total += jnp.sum((x * x).reshape(ROWS // 8, 8, TILE), axis=0)
        spread = jnp.sum(total, axis=0, keepdims=True) * (1.0 / FRAMES)
        scale = lax.rsqrt(spread + epsilon)
        for r in range(0, FRAMES, ROWS):
            x = raw[s, pl.ds(r, ROWS), cols].astype(jnp.float32) - center
            y = x * scale
            scored[s, pl.ds(r, ROWS), cols] = y.astype(jnp.bfloat16)
            if step is not None:
                mine = jnp.where(owner_ref[step] == blk, 1.0, 0.0)
                turned = (y * mine).T.astype(jnp.bfloat16)
                turned = turned.reshape(2, NZ // 2, PIECE, ROWS)
                for i in range(2):
                    at = NZ // 2 * (i + step - 2 * i * step)
                    panel[
                        pl.ds(at, NZ // 2), s * STEPS + step, :, pl.ds(r, ROWS)
                    ] = turned[i]

    rest = [
        (s, c) for s in range(MEMBERS) for c in range(STEPS * PANEL, COLUMNS, TILE)
    ]

    def some_rest(n):
        for _ in range(n):
            if rest:
                standardize(*rest.pop(0), None)

    def far(o, sign):
        return (sign > 0) == (o % 2 == 0)

    SIGNS = (1, -1)
    a_copies = {}

    def send_a(o, sign, t):
        way = 0 if sign > 0 else 1
        j = (yi + o) % NY
        mine = panel.at[(zi + sign * (3 - t) + NZ) % NZ, j]
        if t == 0:
            if far(o, sign):
                a_copies[o, sign, 3] = send(
                    panel.at[(zi + 4) % NZ, j], land_a.at[o, way, 3], at_z(2 * sign)
                )
            src = mine
        else:
            a_copies[o, sign, t - 1].wait_recv()
            src = land_a.at[o, way, t - 1]
            if t == 1 and far(o, sign):
                a_copies[o, sign, 3].wait_recv()
                src[...] += mine[...] + land_a[o, way, 3]
            else:
                src[...] += mine[...]
        a_copies[o, sign, t] = send(src, land_a.at[o, way, t], at_z(sign))

    def step_a(o, t):
        for sign in SIGNS:
            send_a(o, sign, t)

    small[0].wait()
    for i, o in enumerate(order):
        loads[i].wait()
        s, k = (yi + o) % NY // STEPS, (yi + o) % STEPS
        standardize(s, k * PANEL, k)
        if i == 0:
            pl.semaphore_wait(barrier, len(peers))
        if o:
            step_a(o, 0)
    loads[NY].wait()
    some_rest(4)
    step_a(2, 1)
    step_a(0, 0)
    step_a(1, 1)
    step_a(3, 1)
    some_rest(4)
    step_a(2, 2)
    step_a(0, 1)
    step_a(1, 2)
    step_a(3, 2)

    b_copies = {}
    for o in order:
        if o == 1:
            step_a(0, 2)
        for sign in SIGNS:
            a_copies[o, sign, 2].wait_recv()
        mid[o] = panel[zi, (yi + o) % NY] + land_a[o, 0, 2] + land_a[o, 1, 2]
        if o:
            b_copies[o] = send(mid.at[o], land_b.at[o - 1], at_y(o))
    for o in (1, 3, 2):
        b_copies[o].wait_recv()
    whole[zi, yi] = mid[0] + land_b[0] + land_b[1] + land_b[2]
    g_copies, c_copies = {}, {}

    def send_c(o, sign, t):
        if t:
            c_copies[o, sign, t - 1].wait_recv()
        piece = whole.at[(zi - sign * t + NZ) % NZ, (yi - o + NY) % NY]
        if t == 2 and far(o, sign):
            c_copies[o, sign, 3] = send(piece, piece, at_z(2 * sign))
        c_copies[o, sign, t] = send(piece, piece, at_z(sign))

    for o in (2, 1, 3):
        g_copies[o] = send(whole.at[zi, yi], whole.at[zi, yi], at_y(o))
    for sign in SIGNS:
        send_c(0, sign, 0)

    small[1].wait()
    halves = []
    for s in range(MEMBERS):
        label = labels_ref[grp * MEMBERS + s]
        same = jnp.int32(0)
        for i in range(N_GRP * MEMBERS):
            same += jnp.where(labels_ref[i] == label, 1, 0)
        counted = jnp.full((1, WIDE), same.astype(jnp.float32))
        halves.append(0.5 / (COHORTS * counted))

    def compute(offsets, step=None):
        chunks = [(zi + o + NZ) % NZ for o in offsets]
        first, steps = (0, STEPS) if step is None else (step, 1)

        def tile(j, carry):
            cols = pl.ds(pl.multiple_of(j * WIDE, WIDE), WIDE)
            total = None
            for s in range(MEMBERS):
                rows = jnp.concatenate(
                    [
                        whole[d, pl.ds(s * STEPS + first, steps)].reshape(
                            steps * PIECE, FRAMES
                        )
                        for d in chunks
                    ],
                    axis=0,
                )
                q = jnp.dot(
                    rows, scored[s, :, cols], preferred_element_type=jnp.float32
                ) * (1.0 / FRAMES)
                q = jnp.clip(q, -clip_limit, clip_limit)
                term = halves[s] * (jnp.log(1.0 + q) - jnp.log(1.0 - q))
                total = term if total is None else total + term
            total = total.astype(jnp.bfloat16).reshape(
                len(chunks), steps, NC, OUT_ROWS, WIDE
            )
            for i, d in enumerate(chunks):
                for k in range(steps):
                    for c in range(NC):
                        part[d, c, first + k, :, cols] = total[i, k, c]
            return carry

        lax.fori_loop(0, COLUMNS // WIDE, tile, 0)
        mine = pl.ds(first, steps)
        return [
            send(part.at[d, 1 - core, mine], land_e.at[d, mine], other_core)
            for d in chunks
        ]

    base = count[0]
    count[0] += STEPS * (NQ - 1)

    def h_copy(away, d, k):
        at = base + (away - 1) * STEPS + k
        return pltpu.make_async_remote_copy(
            src_ref=half.at[d, k],
            dst_ref=land_h.at[away - 1, k],
            send_sem=send_sem.at[at],
            recv_sem=recv_sem.at[at],
            device_id=at_q(away),
            device_id_type=MESH,
        )

    def forward(offsets, copies, steps=range(STEPS)):
        for o, copy in zip(offsets, copies):
            d = (zi + o + NZ) % NZ
            copy.wait_recv()
            for k in steps:
                half[d, k] = (
                    part[d, core, k].astype(jnp.float32)
                    + land_e[d, k].astype(jnp.float32)
                ).astype(jnp.bfloat16)
                away = (d + NQ // 2 * k - qi + NQ) % NQ

                @pl.when(away != 0)
                def _():
                    h_copy(away, d, k).start()

    def hop(o, t):
        if t == 0:
            g_copies[o].wait_recv()
        for sign in SIGNS:
            send_c(o, sign, t)

    hop(1, 0)
    hop(3, 0)
    hop(0, 1)
    hop(2, 0)
    near = compute((0,))
    hop(1, 1)
    hop(3, 1)
    hop(0, 2)
    hop(2, 1)
    forward((0,), near)
    next_one = compute((1, -1))
    hop(1, 2)
    hop(3, 2)
    hop(2, 2)
    forward((1, -1), next_one)
    next_two = compute((2, -2))
    forward((2, -2), next_two)
    last = []
    for pair in ((1, 3), (0, 2)):
        for o in pair:
            for sign in SIGNS:
                c_copies[o, sign, 2].wait_recv()
                if far(o, sign):
                    c_copies[o, sign, 3].wait_recv()
        k = (yi + pair[0]) % STEPS
        last.append((k, compute((3, -3, 4), k)))
    for k, copies in last:
        forward((3, -3, 4), copies, (k,))

    for k in range(STEPS):
        total = half[(qi + NQ // 2 * k) % NQ, k].astype(jnp.float32)
        for away in range(1, NQ):
            h_copy(away, 0, k).wait_recv()
            total += land_h[away - 1, k].astype(jnp.float32)
        upper = blk >= owner_ref[k]
        out_ref[k] = jnp.where(upper, total, 0.0)

    for copy in near + next_one + next_two + last[0][1] + last[1][1]:
        copy.wait_send()
    for away in range(1, NQ):
        for k in range(STEPS):
            h_copy(away, 0, k).wait_send()
    for copies in (a_copies, b_copies, g_copies, c_copies):
        for copy in copies.values():
            copy.wait_send()


def body(series, labels, panel_owner):
    half_type = jnp.bfloat16
    summed = pl.pallas_call(
        kernel,
        out_shape=jax.ShapeDtypeStruct((STEPS, OUT_ROWS, COLUMNS), jnp.float32),
        in_specs=[pl.BlockSpec(memory_space=pltpu.HBM)] * 3,
        out_specs=pl.BlockSpec(memory_space=pltpu.VMEM),
        scratch_shapes=[
            pltpu.SMEM((N_GRP * MEMBERS,), jnp.int32),
            pltpu.SMEM((STEPS,), jnp.int32),
            pltpu.VMEM((MEMBERS, FRAMES, COLUMNS), half_type),
            pltpu.VMEM((MEMBERS, FRAMES, COLUMNS), half_type),
            pltpu.VMEM((NZ, NY, PIECE, FRAMES), half_type),
            pltpu.VMEM((NY, 2, 4, PIECE, FRAMES), half_type),
            pltpu.VMEM((NY, PIECE, FRAMES), half_type),
            pltpu.VMEM((NY - 1, PIECE, FRAMES), half_type),
            pltpu.VMEM((NZ, NY, PIECE, FRAMES), half_type),
            pltpu.VMEM((NQ, NC, STEPS, OUT_ROWS, COLUMNS), half_type),
            pltpu.VMEM((NQ, STEPS, OUT_ROWS, COLUMNS), half_type),
            pltpu.VMEM((NQ, STEPS, OUT_ROWS, COLUMNS), half_type),
            pltpu.VMEM((NQ - 1, STEPS, OUT_ROWS, COLUMNS), half_type),
            pltpu.SemaphoreType.DMA((NY + 3,)),
            pltpu.SemaphoreType.DMA((N_COPIES,)),
            pltpu.SemaphoreType.DMA((N_COPIES,)),
        ],
        compiler_params=pltpu.CompilerParams(
            collective_id=0, has_side_effects=True, vmem_limit_bytes=60 * 1024 * 1024
        ),
    )(labels, panel_owner, series)
    return summed.astype(half_type)


def solution(mesh):
    in_specs = (P("grp", None, "blk"), P(), P())
    out_specs = P(None, "grp", "blk")
    return jax.shard_map(body, mesh=mesh, in_specs=in_specs, out_specs=out_specs, check_vma=False)
```

```python
import functools

import jax
import jax.numpy as jnp
from jax import lax
from jax.experimental import pallas as pl
from jax.experimental.pallas import tpu as pltpu
from jax.sharding import PartitionSpec as P

MESH = pl.DeviceIdType.MESH
STEPS, PANEL, COHORTS, MEMBERS = 2, 256, 4, 2
FRAMES, COLUMNS = 512, 1536
NZ, NY, NQ, NC = 8, 4, 8, 2
N_GRP, N_BLK = NQ * NC, NZ * NY
PIECE = PANEL // NZ
OUT_ROWS = PANEL // N_GRP
TILE = 256
WIDE = 512
ROWS = 128
epsilon = 1e-05
clip_limit = 0.99

N_COPIES = NY * (7 + 7) + 2 * NY + NQ + 3 + STEPS * NQ


def kernel(
    labels_hbm, owner_hbm, series_ref, out_ref,
    labels_ref, owner_ref, raw, scored, panel, land_a, mid, land_b, found, whole,
    part, land_e, half, land_h, load_sem, send_sem, recv_sem,
):
    grp, blk = lax.axis_index("grp"), lax.axis_index("blk")
    zi, yi = blk // NY, blk % NY
    qi, core = grp // NC, grp % NC

    def at_z(offset):
        return {"blk": ((zi + offset + NZ) % NZ) * NY + yi}

    def at_y(offset):
        return {"grp": qi * NC + 1 - core, "blk": zi * NY + (yi + offset) % NY}

    def at_q(offset):
        return {"grp": ((qi + offset) % NQ) * NC + 1 - core}

    other_core = at_q(0)

    barrier = pltpu.get_barrier_semaphore()
    peers = [at_y(o) for o in (2, 1, 3)]
    peers += [at_z(o) for o in (1, -1, 2, -2)]
    peers += [at_q(o) for o in range(1, NQ)]
    peers += [other_core]
    for peer in peers:
        pl.semaphore_signal(barrier, inc=1, device_id=peer, device_id_type=MESH)

    loads = []
    small = [
        pltpu.make_async_copy(owner_hbm, owner_ref, load_sem.at[NY + 1]),
        pltpu.make_async_copy(labels_hbm, labels_ref, load_sem.at[NY + 2]),
    ]
    for copy in small:
        copy.start()
    order = (2, 1, 3, 0)
    for i, o in enumerate(order):
        s, k = (yi + o) % NY // STEPS, (yi + o) % STEPS
        cols = pl.ds(pl.multiple_of(k * PANEL, PANEL), PANEL)
        loads.append(
            pltpu.make_async_copy(
                series_ref.at[s, :, cols], raw.at[s, :, cols], load_sem.at[i]
            )
        )
        loads[-1].start()
    cols = pl.ds(STEPS * PANEL, COLUMNS - STEPS * PANEL)
    loads.append(
        pltpu.make_async_copy(
            series_ref.at[:, :, cols], raw.at[:, :, cols], load_sem.at[NY]
        )
    )
    loads[-1].start()

    count = [0]

    def send(src, dst, device):
        k = count[0]
        count[0] += 1
        copy = pltpu.make_async_remote_copy(
            src_ref=src,
            dst_ref=dst,
            send_sem=send_sem.at[k],
            recv_sem=recv_sem.at[k],
            device_id=device,
            device_id_type=MESH,
        )
        copy.start()
        return copy

    def standardize(s, start, step):
        cols = pl.ds(pl.multiple_of(start, TILE), TILE)
        total = jnp.zeros((8, TILE), jnp.float32)
        for r in range(0, FRAMES, ROWS):
            x = raw[s, pl.ds(r, ROWS), cols].astype(jnp.float32)
            total += jnp.sum(x.reshape(ROWS // 8, 8, TILE), axis=0)
        center = jnp.sum(total, axis=0, keepdims=True) * (1.0 / FRAMES)
        total = jnp.zeros((8, TILE), jnp.float32)
        for r in range(0, FRAMES, ROWS):
            x = raw[s, pl.ds(r, ROWS), cols].astype(jnp.float32) - center
            total += jnp.sum((x * x).reshape(ROWS // 8, 8, TILE), axis=0)
        spread = jnp.sum(total, axis=0, keepdims=True) * (1.0 / FRAMES)
        scale = lax.rsqrt(spread + epsilon)
        for r in range(0, FRAMES, ROWS):
            x = raw[s, pl.ds(r, ROWS), cols].astype(jnp.float32) - center
            y = x * scale
            scored[s, pl.ds(r, ROWS), cols] = y.astype(jnp.bfloat16)
            if step is not None:
                mine = jnp.where(owner_ref[step] == blk, 1.0, 0.0)
                turned = (y * mine).T.astype(jnp.bfloat16)
                turned = turned.reshape(2, NZ // 2, PIECE, ROWS)
                for i in range(2):
                    at = NZ // 2 * (i + step - 2 * i * step)
                    panel[
                        pl.ds(at, NZ // 2), s * STEPS + step, :, pl.ds(r, ROWS)
                    ] = turned[i]

    rest = [
        (s, c) for s in range(MEMBERS) for c in range(STEPS * PANEL, COLUMNS, TILE)
    ]

    def some_rest(n):
        for _ in range(n):
            if rest:
                standardize(*rest.pop(0), None)

    def far(o, sign):
        return (sign > 0) == (o % 2 == 0)

    SIGNS = (1, -1)
    a_copies = {}

    def send_a(o, sign, t):
        way = 0 if sign > 0 else 1
        j = (yi + o) % NY
        mine = panel.at[(zi + sign * (3 - t) + NZ) % NZ, j]
        if t == 0:
            if far(o, sign):
                a_copies[o, sign, 3] = send(
                    panel.at[(zi + 4) % NZ, j], land_a.at[o, way, 3], at_z(2 * sign)
                )
            src = mine
        else:
            a_copies[o, sign, t - 1].wait_recv()
            src = land_a.at[o, way, t - 1]
            if t == 1 and far(o, sign):
                a_copies[o, sign, 3].wait_recv()
                src[...] += mine[...] + land_a[o, way, 3]
            else:
                src[...] += mine[...]
        a_copies[o, sign, t] = send(src, land_a.at[o, way, t], at_z(sign))

    def step_a(o, t):
        for sign in SIGNS:
            send_a(o, sign, t)

    small[0].wait()
    for i, o in enumerate(order):
        loads[i].wait()
        s, k = (yi + o) % NY // STEPS, (yi + o) % STEPS
        standardize(s, k * PANEL, k)
        if i == 0:
            pl.semaphore_wait(barrier, len(peers))
        if o:
            step_a(o, 0)
    loads[NY].wait()
    some_rest(4)
    step_a(2, 1)
    step_a(0, 0)
    step_a(1, 1)
    step_a(3, 1)
    some_rest(4)
    step_a(2, 2)
    step_a(0, 1)
    step_a(1, 2)
    step_a(3, 2)

    b_copies = {}
    for o in order:
        if o == 1:
            step_a(0, 2)
        for sign in SIGNS:
            a_copies[o, sign, 2].wait_recv()
        mid[o] = panel[zi, (yi + o) % NY] + land_a[o, 0, 2] + land_a[o, 1, 2]
        b_copies[o] = send(mid.at[o], land_b.at[o], at_y(o))
    for o in (1, 3, 2, 0):
        b_copies[o].wait_recv()
    found[...] = land_b[0] + land_b[1] + land_b[2] + land_b[3]
    g_copies, c_copies = {}, {}

    def send_c(o, sign, t):
        if t:
            c_copies[o, sign, t - 1].wait_recv()
        piece = whole.at[(zi - sign * t + NZ) % NZ, (yi - o + NY) % NY]
        if t == 2 and far(o, sign):
            c_copies[o, sign, 3] = send(piece, piece, at_z(2 * sign))
        c_copies[o, sign, t] = send(piece, piece, at_z(sign))

    for o in order:
        g_copies[o] = send(found, whole.at[zi, yi], at_y(o))
    g_copies[0].wait_recv()
    for sign in SIGNS:
        send_c(0, sign, 0)

    small[1].wait()
    halves = []
    for s in range(MEMBERS):
        label = labels_ref[grp * MEMBERS + s]
        same = jnp.int32(0)
        for i in range(N_GRP * MEMBERS):
            same += jnp.where(labels_ref[i] == label, 1, 0)
        counted = jnp.full((1, WIDE), same.astype(jnp.float32))
        halves.append(0.5 / (COHORTS * counted))

    def compute(offsets, step=None):
        chunks = [(zi + o + NZ) % NZ for o in offsets]
        first, steps = (0, STEPS) if step is None else (step, 1)

        def tile(j, carry):
            cols = pl.ds(pl.multiple_of(j * WIDE, WIDE), WIDE)
            total = None
            for s in range(MEMBERS):
                rows = jnp.concatenate(
                    [
                        whole[d, pl.ds(s * STEPS + first, steps)].reshape(
                            steps * PIECE, FRAMES
                        )
                        for d in chunks
                    ],
                    axis=0,
                )
                q = jnp.dot(
                    rows, scored[s, :, cols], preferred_element_type=jnp.float32
                ) * (1.0 / FRAMES)
                q = jnp.clip(q, -clip_limit, clip_limit)
                term = halves[s] * (jnp.log(1.0 + q) - jnp.log(1.0 - q))
                total = term if total is None else total + term
            total = total.astype(jnp.bfloat16).reshape(
                len(chunks), steps, NC, OUT_ROWS, WIDE
            )
            for i, d in enumerate(chunks):
                for k in range(steps):
                    for c in range(NC):
                        part[d, c, first + k, :, cols] = total[i, k, c]
            return carry

        lax.fori_loop(0, COLUMNS // WIDE, tile, 0)
        mine = pl.ds(first, steps)
        return [
            send(part.at[d, core, mine], land_e.at[d, mine], other_core)
            for d in chunks
        ]

    base = count[0]
    count[0] += STEPS * NQ

    def h_copy(away, d, k):
        at = base + away * STEPS + k
        return pltpu.make_async_remote_copy(
            src_ref=half.at[d, k],
            dst_ref=land_h.at[away, k],
            send_sem=send_sem.at[at],
            recv_sem=recv_sem.at[at],
            device_id=at_q(away),
            device_id_type=MESH,
        )

    def forward(offsets, copies, steps=range(STEPS)):
        for o, copy in zip(offsets, copies):
            d = (zi + o + NZ) % NZ
            copy.wait_recv()
            for k in steps:
                half[d, k] = (
                    part[d, 1 - core, k].astype(jnp.float32)
                    + land_e[d, k].astype(jnp.float32)
                ).astype(jnp.bfloat16)
                h_copy((d + NQ // 2 * k - qi + NQ) % NQ, d, k).start()

    def hop(o, t):
        if t == 0:
            g_copies[o].wait_recv()
        for sign in SIGNS:
            send_c(o, sign, t)

    hop(1, 0)
    hop(3, 0)
    hop(0, 1)
    hop(2, 0)
    near = compute((0,))
    hop(1, 1)
    hop(3, 1)
    hop(0, 2)
    hop(2, 1)
    forward((0,), near)
    next_one = compute((1, -1))
    hop(1, 2)
    hop(3, 2)
    hop(2, 2)
    forward((1, -1), next_one)
    next_two = compute((2, -2))
    forward((2, -2), next_two)
    last = []
    for pair in ((1, 3), (0, 2)):
        for o in pair:
            for sign in SIGNS:
                c_copies[o, sign, 2].wait_recv()
                if far(o, sign):
                    c_copies[o, sign, 3].wait_recv()
        k = (yi + pair[0]) % STEPS
        last.append((k, compute((3, -3, 4), k)))
    for k, copies in last:
        forward((3, -3, 4), copies, (k,))

    for k in range(STEPS):
        total = None
        for away in range(NQ):
            h_copy(away, 0, k).wait_recv()
            term = land_h[away, k].astype(jnp.float32)
            total = term if total is None else total + term
        upper = blk >= owner_ref[k]
        out_ref[k] = jnp.where(upper, total, 0.0)

    for copy in near + next_one + next_two + last[0][1] + last[1][1]:
        copy.wait_send()
    for away in range(NQ):
        for k in range(STEPS):
            h_copy(away, 0, k).wait_send()
    for copies in (a_copies, b_copies, g_copies, c_copies):
        for copy in copies.values():
            copy.wait_send()


def body(series, labels, panel_owner):
    half_type = jnp.bfloat16
    summed = pl.pallas_call(
        kernel,
        out_shape=jax.ShapeDtypeStruct((STEPS, OUT_ROWS, COLUMNS), jnp.float32),
        in_specs=[pl.BlockSpec(memory_space=pltpu.HBM)] * 3,
        out_specs=pl.BlockSpec(memory_space=pltpu.VMEM),
        scratch_shapes=[
            pltpu.SMEM((N_GRP * MEMBERS,), jnp.int32),
            pltpu.SMEM((STEPS,), jnp.int32),
            pltpu.VMEM((MEMBERS, FRAMES, COLUMNS), half_type),
            pltpu.VMEM((MEMBERS, FRAMES, COLUMNS), half_type),
            pltpu.VMEM((NZ, NY, PIECE, FRAMES), half_type),
            pltpu.VMEM((NY, 2, 4, PIECE, FRAMES), half_type),
            pltpu.VMEM((NY, PIECE, FRAMES), half_type),
            pltpu.VMEM((NY, PIECE, FRAMES), half_type),
            pltpu.VMEM((PIECE, FRAMES), half_type),
            pltpu.VMEM((NZ, NY, PIECE, FRAMES), half_type),
            pltpu.VMEM((NQ, NC, STEPS, OUT_ROWS, COLUMNS), half_type),
            pltpu.VMEM((NQ, STEPS, OUT_ROWS, COLUMNS), half_type),
            pltpu.VMEM((NQ, STEPS, OUT_ROWS, COLUMNS), half_type),
            pltpu.VMEM((NQ, STEPS, OUT_ROWS, COLUMNS), half_type),
            pltpu.SemaphoreType.DMA((NY + 3,)),
            pltpu.SemaphoreType.DMA((N_COPIES,)),
            pltpu.SemaphoreType.DMA((N_COPIES,)),
        ],
        compiler_params=pltpu.CompilerParams(
            collective_id=0, has_side_effects=True, vmem_limit_bytes=60 * 1024 * 1024
        ),
    )(labels, panel_owner, series)
    return summed.astype(half_type)


def solution(mesh):
    in_specs = (P("grp", None, "blk"), P(), P())
    out_specs = P(None, "grp", "blk")
    return jax.shard_map(body, mesh=mesh, in_specs=in_specs, out_specs=out_specs, check_vma=False)
```

```python
import functools

import jax
import jax.numpy as jnp
from jax import lax
from jax.experimental import pallas as pl
from jax.experimental.pallas import tpu as pltpu
from jax.sharding import PartitionSpec as P

MESH = pl.DeviceIdType.MESH
STEPS, PANEL, COHORTS, MEMBERS = 2, 256, 4, 2
FRAMES, COLUMNS = 512, 1536
NZ, NY, NQ, NC = 8, 4, 8, 2
N_GRP, N_BLK = NQ * NC, NZ * NY
PIECE = PANEL // NZ
OUT_ROWS = PANEL // N_GRP
TILE = 256
WIDE = 512
ROWS = 128
epsilon = 1e-05
clip_limit = 0.99

N_COPIES = NY * (7 + 7) + 2 * NY + NQ + 3 + STEPS * NQ


def kernel(
    labels_hbm, owner_hbm, series_ref, out_ref,
    labels_ref, owner_ref, raw, scored, panel, land_a, mid, land_b, found, whole,
    part, land_e, half, land_h, load_sem, send_sem, recv_sem,
):
    grp, blk = lax.axis_index("grp"), lax.axis_index("blk")
    zi, yi = blk // NY, blk % NY
    qi, core = grp // NC, grp % NC

    def at_z(offset):
        return {"blk": ((zi + offset + NZ) % NZ) * NY + yi}

    def at_y(offset):
        return {"grp": qi * NC + 1 - core, "blk": zi * NY + (yi + offset) % NY}

    def at_q(offset):
        return {"grp": ((qi + offset) % NQ) * NC + 1 - core}

    other_core = at_q(0)

    barrier = pltpu.get_barrier_semaphore()
    peers = [at_y(o) for o in (2, 1, 3)]
    peers += [at_z(o) for o in (1, -1, 2, -2)]
    peers += [at_q(o) for o in range(1, NQ)]
    peers += [other_core]
    for peer in peers:
        pl.semaphore_signal(barrier, inc=1, device_id=peer, device_id_type=MESH)

    loads = []
    small = [
        pltpu.make_async_copy(owner_hbm, owner_ref, load_sem.at[NY + 1]),
        pltpu.make_async_copy(labels_hbm, labels_ref, load_sem.at[NY + 2]),
    ]
    for copy in small:
        copy.start()
    order = (2, 1, 3, 0)
    for i, o in enumerate(order):
        s, k = (yi + o) % NY // STEPS, (yi + o) % STEPS
        cols = pl.ds(pl.multiple_of(k * PANEL, PANEL), PANEL)
        loads.append(
            pltpu.make_async_copy(
                series_ref.at[s, :, cols], raw.at[s, :, cols], load_sem.at[i]
            )
        )
        loads[-1].start()
    cols = pl.ds(STEPS * PANEL, COLUMNS - STEPS * PANEL)
    loads.append(
        pltpu.make_async_copy(
            series_ref.at[:, :, cols], raw.at[:, :, cols], load_sem.at[NY]
        )
    )
    loads[-1].start()

    count = [0]

    def send(src, dst, device):
        k = count[0]
        count[0] += 1
        copy = pltpu.make_async_remote_copy(
            src_ref=src,
            dst_ref=dst,
            send_sem=send_sem.at[k],
            recv_sem=recv_sem.at[k],
            device_id=device,
            device_id_type=MESH,
        )
        copy.start()
        return copy

    def standardize(s, start, step):
        cols = pl.ds(pl.multiple_of(start, TILE), TILE)
        total = jnp.zeros((8, TILE), jnp.float32)
        for r in range(0, FRAMES, ROWS):
            x = raw[s, pl.ds(r, ROWS), cols].astype(jnp.float32)
            total += jnp.sum(x.reshape(ROWS // 8, 8, TILE), axis=0)
        center = jnp.sum(total, axis=0, keepdims=True) * (1.0 / FRAMES)
        total = jnp.zeros((8, TILE), jnp.float32)
        for r in range(0, FRAMES, ROWS):
            x = raw[s, pl.ds(r, ROWS), cols].astype(jnp.float32) - center
            total += jnp.sum((x * x).reshape(ROWS // 8, 8, TILE), axis=0)
        spread = jnp.sum(total, axis=0, keepdims=True) * (1.0 / FRAMES)
        scale = lax.rsqrt(spread + epsilon)
        for r in range(0, FRAMES, ROWS):
            x = raw[s, pl.ds(r, ROWS), cols].astype(jnp.float32) - center
            y = x * scale
            scored[s, pl.ds(r, ROWS), cols] = y.astype(jnp.bfloat16)
            if step is not None:
                mine = jnp.where(owner_ref[step] == blk, 1.0, 0.0)
                turned = (y * mine).T.astype(jnp.bfloat16)
                turned = turned.reshape(2, NZ // 2, PIECE, ROWS)
                for i in range(2):
                    at = NZ // 2 * (i + step - 2 * i * step)
                    panel[
                        pl.ds(at, NZ // 2), s * STEPS + step, :, pl.ds(r, ROWS)
                    ] = turned[i]

    rest = [
        (s, c) for s in range(MEMBERS) for c in range(STEPS * PANEL, COLUMNS, TILE)
    ]

    def some_rest(n):
        for _ in range(n):
            if rest:
                standardize(*rest.pop(0), None)

    def far(o, sign):
        return (sign > 0) == (o % 2 == 0)

    SIGNS = (1, -1)
    a_copies = {}

    def send_a(o, sign, t):
        way = 0 if sign > 0 else 1
        j = (yi + o) % NY
        mine = panel.at[(zi + sign * (3 - t) + NZ) % NZ, j]
        if t == 0:
            if far(o, sign):
                a_copies[o, sign, 3] = send(
                    panel.at[(zi + 4) % NZ, j], land_a.at[o, way, 3], at_z(2 * sign)
                )
            src = mine
        else:
            a_copies[o, sign, t - 1].wait_recv()
            src = land_a.at[o, way, t - 1]
            if t == 1 and far(o, sign):
                a_copies[o, sign, 3].wait_recv()
                src[...] += mine[...] + land_a[o, way, 3]
            else:
                src[...] += mine[...]
        a_copies[o, sign, t] = send(src, land_a.at[o, way, t], at_z(sign))

    def step_a(o, t):
        for sign in SIGNS:
            send_a(o, sign, t)

    small[0].wait()
    for i, o in enumerate(order):
        loads[i].wait()
        s, k = (yi + o) % NY // STEPS, (yi + o) % STEPS
        standardize(s, k * PANEL, k)
        if i == 0:
            pl.semaphore_wait(barrier, len(peers))
        if o:
            step_a(o, 0)
    loads[NY].wait()
    some_rest(4)
    step_a(2, 1)
    step_a(0, 0)
    step_a(1, 1)
    step_a(3, 1)
    some_rest(4)
    step_a(2, 2)
    step_a(0, 1)
    step_a(1, 2)
    step_a(3, 2)

    b_copies = {}
    for o in order:
        if o == 1:
            step_a(0, 2)
        for sign in SIGNS:
            a_copies[o, sign, 2].wait_recv()
        mid[o] = panel[zi, (yi + o) % NY] + land_a[o, 0, 2] + land_a[o, 1, 2]
        b_copies[o] = send(mid.at[o], land_b.at[o], at_y(o))
    for o in (1, 3, 2, 0):
        b_copies[o].wait_recv()
    found[...] = land_b[0] + land_b[1] + land_b[2] + land_b[3]
    g_copies, c_copies = {}, {}

    def send_c(o, sign, t):
        if t:
            c_copies[o, sign, t - 1].wait_recv()
        piece = whole.at[(zi - sign * t + NZ) % NZ, (yi - o + NY) % NY]
        if t == 2 and far(o, sign):
            c_copies[o, sign, 3] = send(piece, piece, at_z(2 * sign))
        c_copies[o, sign, t] = send(piece, piece, at_z(sign))

    for o in order:
        g_copies[o] = send(found, whole.at[zi, yi], at_y(o))
    g_copies[0].wait_recv()
    for sign in SIGNS:
        send_c(0, sign, 0)

    small[1].wait()
    halves = []
    for s in range(MEMBERS):
        label = labels_ref[grp * MEMBERS + s]
        same = jnp.int32(0)
        for i in range(N_GRP * MEMBERS):
            same += jnp.where(labels_ref[i] == label, 1, 0)
        counted = jnp.full((1, WIDE), same.astype(jnp.float32))
        halves.append(0.5 / (COHORTS * counted))

    def compute(offsets, step=None):
        chunks = [(zi + o + NZ) % NZ for o in offsets]
        first, steps = (0, STEPS) if step is None else (step, 1)

        def tile(j, carry):
            cols = pl.ds(pl.multiple_of(j * WIDE, WIDE), WIDE)
            total = None
            for s in range(MEMBERS):
                rows = jnp.concatenate(
                    [
                        whole[d, pl.ds(s * STEPS + first, steps)].reshape(
                            steps * PIECE, FRAMES
                        )
                        for d in chunks
                    ],
                    axis=0,
                )
                q = jnp.dot(
                    rows, scored[s, :, cols], preferred_element_type=jnp.float32
                ) * (1.0 / FRAMES)
                q = jnp.clip(q, -clip_limit, clip_limit)
                term = halves[s] * (jnp.log(1.0 + q) - jnp.log(1.0 - q))
                total = term if total is None else total + term
            total = total.astype(jnp.bfloat16).reshape(
                len(chunks), steps, NC, OUT_ROWS, WIDE
            )
            for i, d in enumerate(chunks):
                for k in range(steps):
                    for c in range(NC):
                        part[d, c, first + k, :, cols] = total[i, k, c]
            return carry

        lax.fori_loop(0, COLUMNS // WIDE, tile, 0)
        mine = pl.ds(first, steps)
        return [
            send(part.at[d, core, mine], land_e.at[d, mine], other_core)
            for d in chunks
        ]

    base = count[0]
    count[0] += STEPS * NQ

    def h_copy(away, d, k):
        at = base + away * STEPS + k
        return pltpu.make_async_remote_copy(
            src_ref=half.at[d, k],
            dst_ref=land_h.at[away, k],
            send_sem=send_sem.at[at],
            recv_sem=recv_sem.at[at],
            device_id=at_q(away),
            device_id_type=MESH,
        )

    def forward(offsets, copies, steps=range(STEPS)):
        for o, copy in zip(offsets, copies):
            d = (zi + o + NZ) % NZ
            copy.wait_recv()
            for k in steps:
                half[d, k] = (
                    part[d, 1 - core, k].astype(jnp.float32)
                    + land_e[d, k].astype(jnp.float32)
                ).astype(jnp.bfloat16)
                h_copy((d + NQ // 2 * k - qi + NQ) % NQ, d, k).start()

    def hop(o, t):
        if t == 0:
            g_copies[o].wait_recv()
        for sign in SIGNS:
            send_c(o, sign, t)

    hop(1, 0)
    hop(3, 0)
    hop(0, 1)
    hop(2, 0)
    near = compute((0,))
    hop(1, 1)
    hop(3, 1)
    hop(0, 2)
    hop(2, 1)
    forward((0,), near)
    hop(1, 2)
    hop(3, 2)
    next_one = compute((1, -1))
    hop(2, 2)
    forward((1, -1), next_one)
    next_two = compute((2, -2))
    forward((2, -2), next_two)
    last = []
    for pair in ((1, 3), (0, 2)):
        for o in pair:
            for sign in SIGNS:
                c_copies[o, sign, 2].wait_recv()
                if far(o, sign):
                    c_copies[o, sign, 3].wait_recv()
        k = (yi + pair[0]) % STEPS
        last.append((k, compute((3, -3, 4), k)))
    for k, copies in last:
        forward((3, -3, 4), copies, (k,))

    for copy in near + next_one + next_two + last[0][1] + last[1][1]:
        copy.wait_send()
    for away in range(NQ):
        for k in range(STEPS):
            h_copy(away, 0, k).wait_send()
    for copies in (a_copies, b_copies, g_copies, c_copies):
        for copy in copies.values():
            copy.wait_send()

    for k in range(STEPS):
        total = None
        for away in range(NQ):
            h_copy(away, 0, k).wait_recv()
            term = land_h[away, k].astype(jnp.float32)
            total = term if total is None else total + term
        upper = blk >= owner_ref[k]
        out_ref[k] = jnp.where(upper, total, 0.0)


def body(series, labels, panel_owner):
    half_type = jnp.bfloat16
    summed = pl.pallas_call(
        kernel,
        out_shape=jax.ShapeDtypeStruct((STEPS, OUT_ROWS, COLUMNS), jnp.float32),
        in_specs=[pl.BlockSpec(memory_space=pltpu.HBM)] * 3,
        out_specs=pl.BlockSpec(memory_space=pltpu.VMEM),
        scratch_shapes=[
            pltpu.SMEM((N_GRP * MEMBERS,), jnp.int32),
            pltpu.SMEM((STEPS,), jnp.int32),
            pltpu.VMEM((MEMBERS, FRAMES, COLUMNS), half_type),
            pltpu.VMEM((MEMBERS, FRAMES, COLUMNS), half_type),
            pltpu.VMEM((NZ, NY, PIECE, FRAMES), half_type),
            pltpu.VMEM((NY, 2, 4, PIECE, FRAMES), half_type),
            pltpu.VMEM((NY, PIECE, FRAMES), half_type),
            pltpu.VMEM((NY, PIECE, FRAMES), half_type),
            pltpu.VMEM((PIECE, FRAMES), half_type),
            pltpu.VMEM((NZ, NY, PIECE, FRAMES), half_type),
            pltpu.VMEM((NQ, NC, STEPS, OUT_ROWS, COLUMNS), half_type),
            pltpu.VMEM((NQ, STEPS, OUT_ROWS, COLUMNS), half_type),
            pltpu.VMEM((NQ, STEPS, OUT_ROWS, COLUMNS), half_type),
            pltpu.VMEM((NQ, STEPS, OUT_ROWS, COLUMNS), half_type),
            pltpu.SemaphoreType.DMA((NY + 3,)),
            pltpu.SemaphoreType.DMA((N_COPIES,)),
            pltpu.SemaphoreType.DMA((N_COPIES,)),
        ],
        compiler_params=pltpu.CompilerParams(
            collective_id=0, has_side_effects=True, vmem_limit_bytes=60 * 1024 * 1024
        ),
    )(labels, panel_owner, series)
    return summed.astype(half_type)


def solution(mesh):
    in_specs = (P("grp", None, "blk"), P(), P())
    out_specs = P(None, "grp", "blk")
    return jax.shard_map(body, mesh=mesh, in_specs=in_specs, out_specs=out_specs, check_vma=False)
```

```python
import functools

import jax
import jax.numpy as jnp
from jax import lax
from jax.experimental import pallas as pl
from jax.experimental.pallas import tpu as pltpu
from jax.sharding import PartitionSpec as P

MESH = pl.DeviceIdType.MESH
STEPS, PANEL, COHORTS, MEMBERS = 2, 256, 4, 2
FRAMES, COLUMNS = 512, 1536
NZ, NY, NQ, NC = 8, 4, 8, 2
N_GRP, N_BLK = NQ * NC, NZ * NY
PIECE = PANEL // NZ
OUT_ROWS = PANEL // N_GRP
TILE = 256
WIDE = 512
ROWS = 128
epsilon = 1e-05
clip_limit = 0.99

N_COPIES = NY * (7 + 7) + 2 * NY + NQ + 3 + STEPS * NQ


def kernel(
    labels_hbm, owner_hbm, series_ref, out_ref,
    labels_ref, owner_ref, raw, scored, panel, land_a, mid, land_b, found, whole,
    part, land_e, half, land_h, load_sem, send_sem, recv_sem,
):
    grp, blk = lax.axis_index("grp"), lax.axis_index("blk")
    zi, yi = blk // NY, blk % NY
    qi, core = grp // NC, grp % NC

    def at_z(offset):
        return {"blk": ((zi + offset + NZ) % NZ) * NY + yi}

    def at_y(offset):
        return {"grp": qi * NC + 1 - core, "blk": zi * NY + (yi + offset) % NY}

    def at_q(offset):
        return {"grp": ((qi + offset) % NQ) * NC + 1 - core}

    other_core = at_q(0)

    barrier = pltpu.get_barrier_semaphore()
    peers = [at_y(o) for o in (2, 1, 3)]
    peers += [at_z(o) for o in (1, -1, 2, -2)]
    peers += [at_q(o) for o in range(1, NQ)]
    peers += [other_core]
    for peer in peers:
        pl.semaphore_signal(barrier, inc=1, device_id=peer, device_id_type=MESH)

    loads = []
    small = [
        pltpu.make_async_copy(owner_hbm, owner_ref, load_sem.at[NY + 1]),
        pltpu.make_async_copy(labels_hbm, labels_ref, load_sem.at[NY + 2]),
    ]
    for copy in small:
        copy.start()
    order = (2, 1, 3, 0)
    for i, o in enumerate(order):
        s, k = (yi + o) % NY // STEPS, (yi + o) % STEPS
        cols = pl.ds(pl.multiple_of(k * PANEL, PANEL), PANEL)
        loads.append(
            pltpu.make_async_copy(
                series_ref.at[s, :, cols], raw.at[s, :, cols], load_sem.at[i]
            )
        )
        loads[-1].start()
    cols = pl.ds(STEPS * PANEL, COLUMNS - STEPS * PANEL)
    loads.append(
        pltpu.make_async_copy(
            series_ref.at[:, :, cols], raw.at[:, :, cols], load_sem.at[NY]
        )
    )
    loads[-1].start()

    count = [0]

    def send(src, dst, device):
        k = count[0]
        count[0] += 1
        copy = pltpu.make_async_remote_copy(
            src_ref=src,
            dst_ref=dst,
            send_sem=send_sem.at[k],
            recv_sem=recv_sem.at[k],
            device_id=device,
            device_id_type=MESH,
        )
        copy.start()
        return copy

    def standardize(s, start, step):
        cols = pl.ds(pl.multiple_of(start, TILE), TILE)
        total = jnp.zeros((8, TILE), jnp.float32)
        for r in range(0, FRAMES, ROWS):
            x = raw[s, pl.ds(r, ROWS), cols].astype(jnp.float32)
            total += jnp.sum(x.reshape(ROWS // 8, 8, TILE), axis=0)
        center = jnp.sum(total, axis=0, keepdims=True) * (1.0 / FRAMES)
        total = jnp.zeros((8, TILE), jnp.float32)
        for r in range(0, FRAMES, ROWS):
            x = raw[s, pl.ds(r, ROWS), cols].astype(jnp.float32) - center
            total += jnp.sum((x * x).reshape(ROWS // 8, 8, TILE), axis=0)
        spread = jnp.sum(total, axis=0, keepdims=True) * (1.0 / FRAMES)
        scale = lax.rsqrt(spread + epsilon)
        for r in range(0, FRAMES, ROWS):
            x = raw[s, pl.ds(r, ROWS), cols].astype(jnp.float32) - center
            y = x * scale
            scored[s, pl.ds(r, ROWS), cols] = y.astype(jnp.bfloat16)
            if step is not None:
                mine = jnp.where(owner_ref[step] == blk, 1.0, 0.0)
                turned = (y * mine).T.astype(jnp.bfloat16)
                turned = turned.reshape(2, NZ // 2, PIECE, ROWS)
                for i in range(2):
                    at = NZ // 2 * (i + step - 2 * i * step)
                    panel[
                        pl.ds(at, NZ // 2), s * STEPS + step, :, pl.ds(r, ROWS)
                    ] = turned[i]

    rest = [
        (s, c) for s in range(MEMBERS) for c in range(STEPS * PANEL, COLUMNS, TILE)
    ]

    def some_rest(n):
        for _ in range(n):
            if rest:
                standardize(*rest.pop(0), None)

    def far(o, sign):
        return (sign > 0) == (o % 2 == 0)

    SIGNS = (1, -1)
    a_copies = {}

    def send_a(o, sign, t):
        way = 0 if sign > 0 else 1
        j = (yi + o) % NY
        mine = panel.at[(zi + sign * (3 - t) + NZ) % NZ, j]
        if t == 0:
            if far(o, sign):
                a_copies[o, sign, 3] = send(
                    panel.at[(zi + 4) % NZ, j], land_a.at[o, way, 3], at_z(2 * sign)
                )
            src = mine
        else:
            a_copies[o, sign, t - 1].wait_recv()
            src = land_a.at[o, way, t - 1]
            if t == 1 and far(o, sign):
                a_copies[o, sign, 3].wait_recv()
                src[...] += mine[...] + land_a[o, way, 3]
            else:
                src[...] += mine[...]
        a_copies[o, sign, t] = send(src, land_a.at[o, way, t], at_z(sign))

    def step_a(o, t):
        for sign in SIGNS:
            send_a(o, sign, t)

    small[0].wait()
    for i, o in enumerate(order):
        loads[i].wait()
        s, k = (yi + o) % NY // STEPS, (yi + o) % STEPS
        standardize(s, k * PANEL, k)
        if i == 0:
            pl.semaphore_wait(barrier, len(peers))
        if o:
            step_a(o, 0)
    loads[NY].wait()
    some_rest(4)
    step_a(2, 1)
    step_a(0, 0)
    step_a(1, 1)
    step_a(3, 1)
    some_rest(4)
    step_a(2, 2)
    step_a(0, 1)
    step_a(1, 2)
    step_a(3, 2)

    b_copies = {}
    for o in order:
        if o == 1:
            step_a(0, 2)
        for sign in SIGNS:
            a_copies[o, sign, 2].wait_recv()
        mid[o] = panel[zi, (yi + o) % NY] + land_a[o, 0, 2] + land_a[o, 1, 2]
        b_copies[o] = send(mid.at[o], land_b.at[o], at_y(o))
    for o in (1, 3, 2, 0):
        b_copies[o].wait_recv()
    found[...] = land_b[0] + land_b[1] + land_b[2] + land_b[3]
    g_copies, c_copies = {}, {}

    def send_c(o, sign, t):
        if t:
            c_copies[o, sign, t - 1].wait_recv()
        piece = whole.at[(zi - sign * t + NZ) % NZ, (yi - o + NY) % NY]
        if t == 2 and far(o, sign):
            c_copies[o, sign, 3] = send(piece, piece, at_z(2 * sign))
        c_copies[o, sign, t] = send(piece, piece, at_z(sign))

    for o in order:
        g_copies[o] = send(found, whole.at[zi, yi], at_y(o))
    g_copies[0].wait_recv()
    for sign in SIGNS:
        send_c(0, sign, 0)

    small[1].wait()
    halves = []
    for s in range(MEMBERS):
        label = labels_ref[grp * MEMBERS + s]
        same = jnp.int32(0)
        for i in range(N_GRP * MEMBERS):
            same += jnp.where(labels_ref[i] == label, 1, 0)
        counted = jnp.full((1, WIDE), same.astype(jnp.float32))
        halves.append(0.5 / (COHORTS * counted))

    def compute(offsets, step=None):
        chunks = [(zi + o + NZ) % NZ for o in offsets]
        first, steps = (0, STEPS) if step is None else (step, 1)

        def tile(j, carry):
            cols = pl.ds(pl.multiple_of(j * WIDE, WIDE), WIDE)
            total = None
            for s in range(MEMBERS):
                rows = jnp.concatenate(
                    [
                        whole[d, pl.ds(s * STEPS + first, steps)].reshape(
                            steps * PIECE, FRAMES
                        )
                        for d in chunks
                    ],
                    axis=0,
                )
                q = jnp.dot(
                    rows, scored[s, :, cols], preferred_element_type=jnp.float32
                ) * (1.0 / FRAMES)
                q = jnp.clip(q, -clip_limit, clip_limit)
                term = halves[s] * (jnp.log(1.0 + q) - jnp.log(1.0 - q))
                total = term if total is None else total + term
            total = total.astype(jnp.bfloat16).reshape(
                len(chunks), steps, NC, OUT_ROWS, WIDE
            )
            for i, d in enumerate(chunks):
                for k in range(steps):
                    for c in range(NC):
                        part[d, c, first + k, :, cols] = total[i, k, c]
            return carry

        lax.fori_loop(0, COLUMNS // WIDE, tile, 0)
        mine = pl.ds(first, steps)
        return [
            send(part.at[d, core, mine], land_e.at[d, mine], other_core)
            for d in chunks
        ]

    base = count[0]
    count[0] += STEPS * NQ

    def h_copy(away, d, k):
        at = base + away * STEPS + k
        return pltpu.make_async_remote_copy(
            src_ref=half.at[d, k],
            dst_ref=land_h.at[away, k],
            send_sem=send_sem.at[at],
            recv_sem=recv_sem.at[at],
            device_id=at_q(away),
            device_id_type=MESH,
        )

    def forward(offsets, copies, steps=range(STEPS)):
        for o, copy in zip(offsets, copies):
            d = (zi + o + NZ) % NZ
            copy.wait_recv()
            for k in steps:
                half[d, k] = (
                    part[d, 1 - core, k].astype(jnp.float32)
                    + land_e[d, k].astype(jnp.float32)
                ).astype(jnp.bfloat16)
                h_copy((d + NQ // 2 * k - qi + NQ) % NQ, d, k).start()

    def hop(o, t):
        if t == 0:
            g_copies[o].wait_recv()
        for sign in SIGNS:
            send_c(o, sign, t)

    hop(1, 0)
    hop(3, 0)
    hop(0, 1)
    hop(2, 0)
    near = compute((0,))
    hop(1, 1)
    hop(3, 1)
    hop(0, 2)
    hop(2, 1)
    forward((0,), near)
    next_one = compute((1, -1))
    hop(1, 2)
    hop(3, 2)
    hop(2, 2)
    forward((1, -1), next_one)
    next_two = compute((2, -2))
    forward((2, -2), next_two)
    last = []
    for pair in ((1, 3), (0, 2)):
        for o in pair:
            for sign in SIGNS:
                c_copies[o, sign, 2].wait_recv()
                if far(o, sign):
                    c_copies[o, sign, 3].wait_recv()
        k = (yi + pair[0]) % STEPS
        last.append((k, compute((3, -3, 4), k)))
    for k, copies in last:
        forward((3, -3, 4), copies, (k,))

    for copy in near + next_one + next_two + last[0][1] + last[1][1]:
        copy.wait_send()
    for away in range(NQ):
        for k in range(STEPS):
            h_copy(away, 0, k).wait_send()
    for copies in (a_copies, b_copies, g_copies, c_copies):
        for copy in copies.values():
            copy.wait_send()

    for k in range(STEPS):
        total = None
        for away in range(NQ):
            h_copy(away, 0, k).wait_recv()
            term = land_h[away, k].astype(jnp.float32)
            total = term if total is None else total + term
        upper = blk >= owner_ref[k]
        out_ref[k] = jnp.where(upper, total, 0.0).astype(out_ref.dtype)


def body(series, labels, panel_owner):
    half_type = jnp.bfloat16
    return pl.pallas_call(
        kernel,
        out_shape=jax.ShapeDtypeStruct((STEPS, OUT_ROWS, COLUMNS), half_type),
        in_specs=[pl.BlockSpec(memory_space=pltpu.HBM)] * 3,
        out_specs=pl.BlockSpec(memory_space=pltpu.VMEM),
        scratch_shapes=[
            pltpu.SMEM((N_GRP * MEMBERS,), jnp.int32),
            pltpu.SMEM((STEPS,), jnp.int32),
            pltpu.VMEM((MEMBERS, FRAMES, COLUMNS), half_type),
            pltpu.VMEM((MEMBERS, FRAMES, COLUMNS), half_type),
            pltpu.VMEM((NZ, NY, PIECE, FRAMES), half_type),
            pltpu.VMEM((NY, 2, 4, PIECE, FRAMES), half_type),
            pltpu.VMEM((NY, PIECE, FRAMES), half_type),
            pltpu.VMEM((NY, PIECE, FRAMES), half_type),
            pltpu.VMEM((PIECE, FRAMES), half_type),
            pltpu.VMEM((NZ, NY, PIECE, FRAMES), half_type),
            pltpu.VMEM((NQ, NC, STEPS, OUT_ROWS, COLUMNS), half_type),
            pltpu.VMEM((NQ, STEPS, OUT_ROWS, COLUMNS), half_type),
            pltpu.VMEM((NQ, STEPS, OUT_ROWS, COLUMNS), half_type),
            pltpu.VMEM((NQ, STEPS, OUT_ROWS, COLUMNS), half_type),
            pltpu.SemaphoreType.DMA((NY + 3,)),
            pltpu.SemaphoreType.DMA((N_COPIES,)),
            pltpu.SemaphoreType.DMA((N_COPIES,)),
        ],
        compiler_params=pltpu.CompilerParams(
            collective_id=0, has_side_effects=True, vmem_limit_bytes=60 * 1024 * 1024
        ),
    )(labels, panel_owner, series)


def solution(mesh):
    in_specs = (P("grp", None, "blk"), P(), P())
    out_specs = P(None, "grp", "blk")
    return jax.shard_map(body, mesh=mesh, in_specs=in_specs, out_specs=out_specs, check_vma=False)
```

```python
import functools

import jax
import jax.numpy as jnp
from jax import lax
from jax.experimental import pallas as pl
from jax.experimental.pallas import tpu as pltpu
from jax.sharding import PartitionSpec as P

MESH = pl.DeviceIdType.MESH
STEPS, PANEL, COHORTS, MEMBERS = 2, 256, 4, 2
FRAMES, COLUMNS = 512, 1536
NZ, NY, NQ, NC = 8, 4, 8, 2
N_GRP, N_BLK = NQ * NC, NZ * NY
PIECE = PANEL // NZ
OUT_ROWS = PANEL // N_GRP
TILE = 256
WIDE = 768
ROWS = 128
epsilon = 1e-05
clip_limit = 0.99

N_COPIES = NY * (7 + 7) + 2 * NY + NQ + 3 + STEPS * NQ


def kernel(
    labels_hbm, owner_hbm, series_ref, out_ref,
    labels_ref, owner_ref, raw, scored, panel, land_a, mid, land_b, found, whole,
    part, land_e, half, land_h, load_sem, send_sem, recv_sem,
):
    grp, blk = lax.axis_index("grp"), lax.axis_index("blk")
    zi, yi = blk // NY, blk % NY
    qi, core = grp // NC, grp % NC

    def at_z(offset):
        return {"blk": ((zi + offset + NZ) % NZ) * NY + yi}

    def at_y(offset):
        return {"grp": qi * NC + 1 - core, "blk": zi * NY + (yi + offset) % NY}

    def at_q(offset):
        return {"grp": ((qi + offset) % NQ) * NC + 1 - core}

    other_core = at_q(0)

    barrier = pltpu.get_barrier_semaphore()
    peers = [at_y(o) for o in (2, 1, 3)]
    peers += [at_z(o) for o in (1, -1, 2, -2)]
    peers += [at_q(o) for o in range(1, NQ)]
    peers += [other_core]
    for peer in peers:
        pl.semaphore_signal(barrier, inc=1, device_id=peer, device_id_type=MESH)

    loads = []
    small = [
        pltpu.make_async_copy(owner_hbm, owner_ref, load_sem.at[NY + 1]),
        pltpu.make_async_copy(labels_hbm, labels_ref, load_sem.at[NY + 2]),
    ]
    for copy in small:
        copy.start()
    order = (2, 1, 3, 0)
    for i, o in enumerate(order):
        s, k = (yi + o) % NY // STEPS, (yi + o) % STEPS
        cols = pl.ds(pl.multiple_of(k * PANEL, PANEL), PANEL)
        loads.append(
            pltpu.make_async_copy(
                series_ref.at[s, :, cols], raw.at[s, :, cols], load_sem.at[i]
            )
        )
        loads[-1].start()
    cols = pl.ds(STEPS * PANEL, COLUMNS - STEPS * PANEL)
    loads.append(
        pltpu.make_async_copy(
            series_ref.at[:, :, cols], raw.at[:, :, cols], load_sem.at[NY]
        )
    )
    loads[-1].start()

    count = [0]

    def send(src, dst, device):
        k = count[0]
        count[0] += 1
        copy = pltpu.make_async_remote_copy(
            src_ref=src,
            dst_ref=dst,
            send_sem=send_sem.at[k],
            recv_sem=recv_sem.at[k],
            device_id=device,
            device_id_type=MESH,
        )
        copy.start()
        return copy

    def standardize(s, start, step):
        cols = pl.ds(pl.multiple_of(start, TILE), TILE)
        total = jnp.zeros((8, TILE), jnp.float32)
        for r in range(0, FRAMES, ROWS):
            x = raw[s, pl.ds(r, ROWS), cols].astype(jnp.float32)
            total += jnp.sum(x.reshape(ROWS // 8, 8, TILE), axis=0)
        center = jnp.sum(total, axis=0, keepdims=True) * (1.0 / FRAMES)
        total = jnp.zeros((8, TILE), jnp.float32)
        for r in range(0, FRAMES, ROWS):
            x = raw[s, pl.ds(r, ROWS), cols].astype(jnp.float32) - center
            total += jnp.sum((x * x).reshape(ROWS // 8, 8, TILE), axis=0)
        spread = jnp.sum(total, axis=0, keepdims=True) * (1.0 / FRAMES)
        scale = lax.rsqrt(spread + epsilon)
        for r in range(0, FRAMES, ROWS):
            x = raw[s, pl.ds(r, ROWS), cols].astype(jnp.float32) - center
            y = x * scale
            scored[s, pl.ds(r, ROWS), cols] = y.astype(jnp.bfloat16)
            if step is not None:
                mine = jnp.where(owner_ref[step] == blk, 1.0, 0.0)
                turned = (y * mine).T.astype(jnp.bfloat16)
                turned = turned.reshape(2, NZ // 2, PIECE, ROWS)
                for i in range(2):
                    at = NZ // 2 * (i + step - 2 * i * step)
                    panel[
                        pl.ds(at, NZ // 2), s * STEPS + step, :, pl.ds(r, ROWS)
                    ] = turned[i]

    rest = [
        (s, c) for s in range(MEMBERS) for c in range(STEPS * PANEL, COLUMNS, TILE)
    ]

    def some_rest(n):
        for _ in range(n):
            if rest:
                standardize(*rest.pop(0), None)

    def far(o, sign):
        return (sign > 0) == (o % 2 == 0)

    SIGNS = (1, -1)
    a_copies = {}

    def reach(o, sign):
        return 4 if o == 0 and far(o, sign) else 3

    def send_a(o, sign, t):
        way = 0 if sign > 0 else 1
        j = (yi + o) % NY
        mine = panel.at[(zi + sign * (reach(o, sign) - t) + NZ) % NZ, j]
        jump = o != 0 and far(o, sign)
        if t == 0:
            if jump:
                a_copies[o, sign, 3] = send(
                    panel.at[(zi + 4) % NZ, j], land_a.at[o, way, 3], at_z(2 * sign)
                )
            src = mine
        else:
            a_copies[o, sign, t - 1].wait_recv()
            src = land_a.at[o, way, t - 1]
            if t == 1 and jump:
                a_copies[o, sign, 3].wait_recv()
                src[...] += mine[...] + land_a[o, way, 3]
            else:
                src[...] += mine[...]
        a_copies[o, sign, t] = send(src, land_a.at[o, way, t], at_z(sign))

    def step_a(o, t):
        for sign in SIGNS:
            send_a(o, sign, t)

    small[0].wait()
    for i, o in enumerate(order):
        loads[i].wait()
        s, k = (yi + o) % NY // STEPS, (yi + o) % STEPS
        standardize(s, k * PANEL, k)
        if i == 0:
            pl.semaphore_wait(barrier, len(peers))
        if o:
            step_a(o, 0)
    loads[NY].wait()
    some_rest(4)
    step_a(2, 1)
    step_a(0, 0)
    step_a(1, 1)
    step_a(3, 1)
    some_rest(4)
    step_a(2, 2)
    step_a(0, 1)
    step_a(1, 2)
    step_a(3, 2)

    b_copies = {}
    for o in order:
        if o == 1:
            step_a(0, 2)
        if o == 0:
            for sign in SIGNS:
                if far(0, sign):
                    send_a(0, sign, 3)
        total = panel[zi, (yi + o) % NY]
        for way, sign in enumerate(SIGNS):
            t = reach(o, sign) - 1
            a_copies[o, sign, t].wait_recv()
            total += land_a[o, way, t]
        mid[o] = total
        b_copies[o] = send(mid.at[o], land_b.at[o], at_y(o))
    for o in (1, 3, 2, 0):
        b_copies[o].wait_recv()
    found[...] = land_b[0] + land_b[1] + land_b[2] + land_b[3]
    g_copies, c_copies = {}, {}

    def send_c(o, sign, t):
        if t:
            c_copies[o, sign, t - 1].wait_recv()
        piece = whole.at[(zi - sign * t + NZ) % NZ, (yi - o + NY) % NY]
        if o and t == 2 and far(o, sign):
            c_copies[o, sign, 3] = send(piece, piece, at_z(2 * sign))
        c_copies[o, sign, t] = send(piece, piece, at_z(sign))

    for o in order:
        g_copies[o] = send(found, whole.at[zi, yi], at_y(o))
    g_copies[0].wait_recv()
    for sign in SIGNS:
        send_c(0, sign, 0)

    small[1].wait()
    halves = []
    for s in range(MEMBERS):
        label = labels_ref[grp * MEMBERS + s]
        same = jnp.int32(0)
        for i in range(N_GRP * MEMBERS):
            same += jnp.where(labels_ref[i] == label, 1, 0)
        counted = jnp.full((1, WIDE), same.astype(jnp.float32))
        halves.append(0.5 / (COHORTS * counted))

    def compute(offsets, step=None):
        chunks = [(zi + o + NZ) % NZ for o in offsets]
        first, steps = (0, STEPS) if step is None else (step, 1)

        def tile(j, carry):
            cols = pl.ds(pl.multiple_of(j * WIDE, WIDE), WIDE)
            total = None
            for s in range(MEMBERS):
                rows = jnp.concatenate(
                    [
                        whole[d, pl.ds(s * STEPS + first, steps)].reshape(
                            steps * PIECE, FRAMES
                        )
                        for d in chunks
                    ],
                    axis=0,
                )
                q = jnp.dot(
                    rows, scored[s, :, cols], preferred_element_type=jnp.float32
                ) * (1.0 / FRAMES)
                q = jnp.clip(q, -clip_limit, clip_limit)
                term = halves[s] * (jnp.log(1.0 + q) - jnp.log(1.0 - q))
                total = term if total is None else total + term
            total = total.astype(jnp.bfloat16).reshape(
                len(chunks), steps, NC, OUT_ROWS, WIDE
            )
            for i, d in enumerate(chunks):
                for k in range(steps):
                    for c in range(NC):
                        part[d, c, first + k, :, cols] = total[i, k, c]
            return carry

        lax.fori_loop(0, COLUMNS // WIDE, tile, 0)
        mine = pl.ds(first, steps)
        return [
            send(part.at[d, core, mine], land_e.at[d, mine], other_core)
            for d in chunks
        ]

    base = count[0]
    count[0] += STEPS * NQ

    def h_copy(away, d, k):
        at = base + away * STEPS + k
        return pltpu.make_async_remote_copy(
            src_ref=half.at[d, k],
            dst_ref=land_h.at[away, k],
            send_sem=send_sem.at[at],
            recv_sem=recv_sem.at[at],
            device_id=at_q(away),
            device_id_type=MESH,
        )

    def forward(offsets, copies, steps=range(STEPS)):
        for o, copy in zip(offsets, copies):
            d = (zi + o + NZ) % NZ
            copy.wait_recv()
            for k in steps:
                half[d, k] = (
                    part[d, 1 - core, k].astype(jnp.float32)
                    + land_e[d, k].astype(jnp.float32)
                ).astype(jnp.bfloat16)
                h_copy((d + NQ // 2 * k - qi + NQ) % NQ, d, k).start()

    def hop(o, t):
        if t == 0:
            g_copies[o].wait_recv()
        for sign in SIGNS:
            send_c(o, sign, t)

    hop(1, 0)
    hop(3, 0)
    hop(0, 1)
    hop(2, 0)
    near = compute((0,))
    hop(1, 1)
    hop(3, 1)
    hop(0, 2)
    hop(2, 1)
    forward((0,), near)
    next_one = compute((1, -1))
    hop(1, 2)
    hop(3, 2)
    hop(2, 2)
    forward((1, -1), next_one)
    next_two = compute((2, -2))
    for sign in SIGNS:
        if far(0, sign):
            send_c(0, sign, 3)
    forward((2, -2), next_two)
    last = []
    for pair in ((1, 3), (0, 2)):
        for o in pair:
            for sign in SIGNS:
                if reach(o, sign) == 3:
                    c_copies[o, sign, 2].wait_recv()
                if far(o, sign):
                    c_copies[o, sign, 3].wait_recv()
        k = (yi + pair[0]) % STEPS
        last.append((k, compute((3, -3, 4), k)))
    for k, copies in last:
        forward((3, -3, 4), copies, (k,))

    for copy in near + next_one + next_two + last[0][1] + last[1][1]:
        copy.wait_send()
    for away in range(NQ):
        for k in range(STEPS):
            h_copy(away, 0, k).wait_send()
    for copies in (a_copies, b_copies, g_copies, c_copies):
        for copy in copies.values():
            copy.wait_send()

    for k in range(STEPS):
        total = None
        for away in range(NQ):
            h_copy(away, 0, k).wait_recv()
            term = land_h[away, k].astype(jnp.float32)
            total = term if total is None else total + term
        upper = blk >= owner_ref[k]
        out_ref[k] = jnp.where(upper, total, 0.0).astype(out_ref.dtype)


def body(series, labels, panel_owner):
    half_type = jnp.bfloat16
    return pl.pallas_call(
        kernel,
        out_shape=jax.ShapeDtypeStruct((STEPS, OUT_ROWS, COLUMNS), half_type),
        in_specs=[pl.BlockSpec(memory_space=pltpu.HBM)] * 3,
        out_specs=pl.BlockSpec(memory_space=pltpu.VMEM),
        scratch_shapes=[
            pltpu.SMEM((N_GRP * MEMBERS,), jnp.int32),
            pltpu.SMEM((STEPS,), jnp.int32),
            pltpu.VMEM((MEMBERS, FRAMES, COLUMNS), half_type),
            pltpu.VMEM((MEMBERS, FRAMES, COLUMNS), half_type),
            pltpu.VMEM((NZ, NY, PIECE, FRAMES), half_type),
            pltpu.VMEM((NY, 2, 4, PIECE, FRAMES), half_type),
            pltpu.VMEM((NY, PIECE, FRAMES), half_type),
            pltpu.VMEM((NY, PIECE, FRAMES), half_type),
            pltpu.VMEM((PIECE, FRAMES), half_type),
            pltpu.VMEM((NZ, NY, PIECE, FRAMES), half_type),
            pltpu.VMEM((NQ, NC, STEPS, OUT_ROWS, COLUMNS), half_type),
            pltpu.VMEM((NQ, STEPS, OUT_ROWS, COLUMNS), half_type),
            pltpu.VMEM((NQ, STEPS, OUT_ROWS, COLUMNS), half_type),
            pltpu.VMEM((NQ, STEPS, OUT_ROWS, COLUMNS), half_type),
            pltpu.SemaphoreType.DMA((NY + 3,)),
            pltpu.SemaphoreType.DMA((N_COPIES,)),
            pltpu.SemaphoreType.DMA((N_COPIES,)),
        ],
        compiler_params=pltpu.CompilerParams(
            collective_id=0, has_side_effects=True, vmem_limit_bytes=60 * 1024 * 1024
        ),
    )(labels, panel_owner, series)


def solution(mesh):
    in_specs = (P("grp", None, "blk"), P(), P())
    out_specs = P(None, "grp", "blk")
    return jax.shard_map(body, mesh=mesh, in_specs=in_specs, out_specs=out_specs, check_vma=False)
```

```python
import functools

import jax
import jax.numpy as jnp
from jax import lax
from jax.experimental import pallas as pl
from jax.experimental.pallas import tpu as pltpu
from jax.sharding import PartitionSpec as P

MESH = pl.DeviceIdType.MESH
STEPS, PANEL, COHORTS, MEMBERS = 2, 256, 4, 2
FRAMES, COLUMNS = 512, 1536
NZ, NY, NQ, NC = 8, 4, 8, 2
N_GRP, N_BLK = NQ * NC, NZ * NY
PIECE = PANEL // NZ
OUT_ROWS = PANEL // N_GRP
TILE = 256
WIDE = 768
ROWS = 128
epsilon = 1e-05
clip_limit = 0.99

N_COPIES = NY * (7 + 7) + 2 * NY + NQ + 3 + STEPS * NQ


def kernel(
    labels_hbm, owner_hbm, series_ref, out_ref,
    labels_ref, owner_ref, raw, scored, panel, land_a, mid, land_b, found, whole,
    part, land_e, half, land_h, load_sem, send_sem, recv_sem,
):
    grp, blk = lax.axis_index("grp"), lax.axis_index("blk")
    zi, yi = blk // NY, blk % NY
    qi, core = grp // NC, grp % NC

    def at_z(offset):
        return {"blk": ((zi + offset + NZ) % NZ) * NY + yi}

    def at_y(offset):
        return {"grp": qi * NC + 1 - core, "blk": zi * NY + (yi + offset) % NY}

    def at_q(offset):
        return {"grp": ((qi + offset) % NQ) * NC + 1 - core}

    other_core = at_q(0)

    barrier = pltpu.get_barrier_semaphore()
    peers = [at_y(o) for o in (2, 1, 3)]
    peers += [at_z(o) for o in (1, -1, 2, -2)]
    peers += [at_q(o) for o in range(1, NQ)]
    peers += [other_core]

    def greet(some):
        for peer in some:
            pl.semaphore_signal(barrier, inc=1, device_id=peer, device_id_type=MESH)

    greet(peers[:7])

    loads = []
    small = [
        pltpu.make_async_copy(owner_hbm, owner_ref, load_sem.at[NY + 1]),
        pltpu.make_async_copy(labels_hbm, labels_ref, load_sem.at[NY + 2]),
    ]
    small[0].start()
    order = (2, 1, 3, 0)
    for i, o in enumerate(order):
        s, k = (yi + o) % NY // STEPS, (yi + o) % STEPS
        cols = pl.ds(pl.multiple_of(k * PANEL, PANEL), PANEL)
        loads.append(
            pltpu.make_async_copy(
                series_ref.at[s, :, cols], raw.at[s, :, cols], load_sem.at[i]
            )
        )
        loads[-1].start()
        if i == 0:
            greet(peers[7:])
    small[1].start()
    cols = pl.ds(STEPS * PANEL, COLUMNS - STEPS * PANEL)
    loads.append(
        pltpu.make_async_copy(
            series_ref.at[:, :, cols], raw.at[:, :, cols], load_sem.at[NY]
        )
    )
    loads[-1].start()

    count = [0]

    def send(src, dst, device):
        k = count[0]
        count[0] += 1
        copy = pltpu.make_async_remote_copy(
            src_ref=src,
            dst_ref=dst,
            send_sem=send_sem.at[k],
            recv_sem=recv_sem.at[k],
            device_id=device,
            device_id_type=MESH,
        )
        copy.start()
        return copy

    def standardize(s, start, step):
        cols = pl.ds(pl.multiple_of(start, TILE), TILE)
        total = jnp.zeros((8, TILE), jnp.float32)
        for r in range(0, FRAMES, ROWS):
            x = raw[s, pl.ds(r, ROWS), cols].astype(jnp.float32)
            total += jnp.sum(x.reshape(ROWS // 8, 8, TILE), axis=0)
        center = jnp.sum(total, axis=0, keepdims=True) * (1.0 / FRAMES)
        total = jnp.zeros((8, TILE), jnp.float32)
        for r in range(0, FRAMES, ROWS):
            x = raw[s, pl.ds(r, ROWS), cols].astype(jnp.float32) - center
            total += jnp.sum((x * x).reshape(ROWS // 8, 8, TILE), axis=0)
        spread = jnp.sum(total, axis=0, keepdims=True) * (1.0 / FRAMES)
        scale = lax.rsqrt(spread + epsilon)
        for r in range(0, FRAMES, ROWS):
            x = raw[s, pl.ds(r, ROWS), cols].astype(jnp.float32) - center
            y = x * scale
            scored[s, pl.ds(r, ROWS), cols] = y.astype(jnp.bfloat16)
            if step is not None:
                mine = jnp.where(owner_ref[step] == blk, 1.0, 0.0)
                turned = (y * mine).T.astype(jnp.bfloat16)
                turned = turned.reshape(2, NZ // 2, PIECE, ROWS)
                for i in range(2):
                    at = NZ // 2 * (i + step - 2 * i * step)
                    panel[
                        pl.ds(at, NZ // 2), s * STEPS + step, :, pl.ds(r, ROWS)
                    ] = turned[i]

    rest = [
        (s, c) for s in range(MEMBERS) for c in range(STEPS * PANEL, COLUMNS, TILE)
    ]

    def some_rest(n):
        for _ in range(n):
            if rest:
                standardize(*rest.pop(0), None)

    def far(o, sign):
        return (sign > 0) == (o % 2 == 0)

    SIGNS = (1, -1)
    a_copies = {}

    def send_a(o, sign, t):
        way = 0 if sign > 0 else 1
        j = (yi + o) % NY
        mine = panel.at[(zi + sign * (3 - t) + NZ) % NZ, j]
        if t == 0:
            if far(o, sign):
                a_copies[o, sign, 3] = send(
                    panel.at[(zi + 4) % NZ, j], land_a.at[o, way, 3], at_z(2 * sign)
                )
            src = mine
        else:
            a_copies[o, sign, t - 1].wait_recv()
            src = land_a.at[o, way, t - 1]
            if t == 1 and far(o, sign):
                a_copies[o, sign, 3].wait_recv()
                src[...] += mine[...] + land_a[o, way, 3]
            else:
                src[...] += mine[...]
        a_copies[o, sign, t] = send(src, land_a.at[o, way, t], at_z(sign))

    def step_a(o, t):
        for sign in SIGNS:
            send_a(o, sign, t)

    small[0].wait()
    for i, o in enumerate(order):
        loads[i].wait()
        s, k = (yi + o) % NY // STEPS, (yi + o) % STEPS
        standardize(s, k * PANEL, k)
        if i == 0:
            pl.semaphore_wait(barrier, len(peers))
        if o:
            step_a(o, 0)
    loads[NY].wait()
    some_rest(4)
    step_a(2, 1)
    step_a(0, 0)
    step_a(1, 1)
    step_a(3, 1)
    some_rest(4)
    step_a(2, 2)
    step_a(0, 1)
    step_a(1, 2)
    step_a(3, 2)

    b_copies = {}
    for o in order:
        if o == 1:
            step_a(0, 2)
        for sign in SIGNS:
            a_copies[o, sign, 2].wait_recv()
        mid[o] = panel[zi, (yi + o) % NY] + land_a[o, 0, 2] + land_a[o, 1, 2]
        b_copies[o] = send(mid.at[o], land_b.at[o], at_y(o))
    for o in (1, 3, 2, 0):
        b_copies[o].wait_recv()
    found[...] = land_b[0] + land_b[1] + land_b[2] + land_b[3]
    g_copies, c_copies = {}, {}

    def send_c(o, sign, t):
        if t:
            c_copies[o, sign, t - 1].wait_recv()
        piece = whole.at[(zi - sign * t + NZ) % NZ, (yi - o + NY) % NY]
        if t == 2 and far(o, sign):
            c_copies[o, sign, 3] = send(piece, piece, at_z(2 * sign))
        c_copies[o, sign, t] = send(piece, piece, at_z(sign))

    for o in order:
        g_copies[o] = send(found, whole.at[zi, yi], at_y(o))
    g_copies[0].wait_recv()
    for sign in SIGNS:
        send_c(0, sign, 0)

    small[1].wait()
    halves = []
    for s in range(MEMBERS):
        label = labels_ref[grp * MEMBERS + s]
        same = jnp.int32(0)
        for i in range(N_GRP * MEMBERS):
            same += jnp.where(labels_ref[i] == label, 1, 0)
        counted = jnp.full((1, WIDE), same.astype(jnp.float32))
        halves.append(0.5 / (COHORTS * counted))

    def compute(offsets, step=None):
        chunks = [(zi + o + NZ) % NZ for o in offsets]
        first, steps = (0, STEPS) if step is None else (step, 1)

        def tile(j, carry):
            cols = pl.ds(pl.multiple_of(j * WIDE, WIDE), WIDE)
            total = None
            for s in range(MEMBERS):
                rows = jnp.concatenate(
                    [
                        whole[d, pl.ds(s * STEPS + first, steps)].reshape(
                            steps * PIECE, FRAMES
                        )
                        for d in chunks
                    ],
                    axis=0,
                )
                q = jnp.dot(
                    rows, scored[s, :, cols], preferred_element_type=jnp.float32
                ) * (1.0 / FRAMES)
                q = jnp.clip(q, -clip_limit, clip_limit)
                term = halves[s] * (jnp.log(1.0 + q) - jnp.log(1.0 - q))
                total = term if total is None else total + term
            total = total.astype(jnp.bfloat16).reshape(
                len(chunks), steps, NC, OUT_ROWS, WIDE
            )
            for i, d in enumerate(chunks):
                for k in range(steps):
                    for c in range(NC):
                        part[d, c, first + k, :, cols] = total[i, k, c]
            return carry

        lax.fori_loop(0, COLUMNS // WIDE, tile, 0)
        mine = pl.ds(first, steps)
        return [
            send(part.at[d, core, mine], land_e.at[d, mine], other_core)
            for d in chunks
        ]

    base = count[0]
    count[0] += STEPS * NQ

    def h_copy(away, d, k):
        at = base + away * STEPS + k
        return pltpu.make_async_remote_copy(
            src_ref=half.at[d, k],
            dst_ref=land_h.at[away, k],
            send_sem=send_sem.at[at],
            recv_sem=recv_sem.at[at],
            device_id=at_q(away),
            device_id_type=MESH,
        )

    def forward(offsets, copies, steps=range(STEPS)):
        for o, copy in zip(offsets, copies):
            d = (zi + o + NZ) % NZ
            copy.wait_recv()
            for k in steps:
                half[d, k] = (
                    part[d, 1 - core, k].astype(jnp.float32)
                    + land_e[d, k].astype(jnp.float32)
                ).astype(jnp.bfloat16)
                h_copy((d + NQ // 2 * k - qi + NQ) % NQ, d, k).start()

    def hop(o, t):
        if t == 0:
            g_copies[o].wait_recv()
        for sign in SIGNS:
            send_c(o, sign, t)

    hop(1, 0)
    hop(3, 0)
    hop(0, 1)
    hop(2, 0)
    near = compute((0,))
    hop(1, 1)
    hop(3, 1)
    hop(0, 2)
    hop(2, 1)
    forward((0,), near)
    next_one = compute((1, -1))
    hop(1, 2)
    hop(3, 2)
    hop(2, 2)
    forward((1, -1), next_one)
    next_two = compute((2, -2))
    forward((2, -2), next_two)
    last = []
    for pair in ((1, 3), (0, 2)):
        for o in pair:
            for sign in SIGNS:
                c_copies[o, sign, 2].wait_recv()
                if far(o, sign):
                    c_copies[o, sign, 3].wait_recv()
        k = (yi + pair[0]) % STEPS
        last.append((k, compute((3, -3, 4), k)))
    for k, copies in last:
        forward((3, -3, 4), copies, (k,))

    for copy in near + next_one + next_two + last[0][1] + last[1][1]:
        copy.wait_send()
    for away in range(NQ):
        for k in range(STEPS):
            h_copy(away, 0, k).wait_send()
    for copies in (a_copies, b_copies, g_copies, c_copies):
        for copy in copies.values():
            copy.wait_send()

    for k in range(STEPS):
        total = None
        for away in range(NQ):
            h_copy(away, 0, k).wait_recv()
            term = land_h[away, k].astype(jnp.float32)
            total = term if total is None else total + term
        upper = blk >= owner_ref[k]
        out_ref[k] = jnp.where(upper, total, 0.0).astype(out_ref.dtype)


def body(series, labels, panel_owner):
    half_type = jnp.bfloat16
    return pl.pallas_call(
        kernel,
        out_shape=jax.ShapeDtypeStruct((STEPS, OUT_ROWS, COLUMNS), half_type),
        in_specs=[pl.BlockSpec(memory_space=pltpu.HBM)] * 3,
        out_specs=pl.BlockSpec(memory_space=pltpu.VMEM),
        scratch_shapes=[
            pltpu.SMEM((N_GRP * MEMBERS,), jnp.int32),
            pltpu.SMEM((STEPS,), jnp.int32),
            pltpu.VMEM((MEMBERS, FRAMES, COLUMNS), half_type),
            pltpu.VMEM((MEMBERS, FRAMES, COLUMNS), half_type),
            pltpu.VMEM((NZ, NY, PIECE, FRAMES), half_type),
            pltpu.VMEM((NY, 2, 4, PIECE, FRAMES), half_type),
            pltpu.VMEM((NY, PIECE, FRAMES), half_type),
            pltpu.VMEM((NY, PIECE, FRAMES), half_type),
            pltpu.VMEM((PIECE, FRAMES), half_type),
            pltpu.VMEM((NZ, NY, PIECE, FRAMES), half_type),
            pltpu.VMEM((NQ, NC, STEPS, OUT_ROWS, COLUMNS), half_type),
            pltpu.VMEM((NQ, STEPS, OUT_ROWS, COLUMNS), half_type),
            pltpu.VMEM((NQ, STEPS, OUT_ROWS, COLUMNS), half_type),
            pltpu.VMEM((NQ, STEPS, OUT_ROWS, COLUMNS), half_type),
            pltpu.SemaphoreType.DMA((NY + 3,)),
            pltpu.SemaphoreType.DMA((N_COPIES,)),
            pltpu.SemaphoreType.DMA((N_COPIES,)),
        ],
        compiler_params=pltpu.CompilerParams(
            collective_id=0, has_side_effects=True, vmem_limit_bytes=60 * 1024 * 1024
        ),
    )(labels, panel_owner, series)


def solution(mesh):
    in_specs = (P("grp", None, "blk"), P(), P())
    out_specs = P(None, "grp", "blk")
    return jax.shard_map(body, mesh=mesh, in_specs=in_specs, out_specs=out_specs, check_vma=False)
```
